256 devices in a mesh: row: 32 (over z, x), col: 8 (over y, core).
Axes of the slice: x: 4, y: 4, z: 8, core: 2. Of those that a mesh axis runs over, the one named last changes fastest.
Arguments:
- sources: float32 [128, 65536], P('col', 'row'), may hold values from -6 to 6
- tiles: bfloat16 [32, 8, 48, 256, 256], P('row', 'col')
- tile_row: int32 [32, 8, 48], P('row', 'col'), may hold values from 0 to 7
- tile_col: int32 [32, 8, 48], P('row', 'col'), may hold values from 0 to 31
- tile_count: int32 [32, 8], P('row', 'col'), may hold values from 1 to 48, as said below
Outputs:
- potential: float32 [128, 65536], P('col', 'row')
The draws below stay inside these ranges and needn't reach their ends.
Inputs may be any that keep to these rules, and one draw needn't show every extreme that they name: `tile_count`: slots at or past a device's count hold no part of the operator; some device holds exactly 48 live slots; tile pairs may repeat and then add.
All inputs are finite; a program needn't handle non-finite values.
Results may differ from the reference program's by a relative error of at most 0.0029.
Values may be sent and summed in bfloat16 or wider, within the bound.
A program may use at most 128 MiB of HBM per device.

```python
import math
import jax
import jax.numpy as jnp
import numpy as np
from jax import lax

TILE = 256
R = 128
RB = 8
TPD = 48
NB = 256
CB = 32
NP = 65536
N_ROW = 32
N_COL = 8


def draw_tiles(key, part):
    base_key = jax.random.fold_in(key, 11)
    tile_shape = (N_ROW, N_COL, TPD, TILE, TILE)
    entries = jax.random.normal(base_key, tile_shape, jnp.float32)
    first_index = jnp.arange(TILE) == 0
    coarse_mask = first_index[:, None] | first_index[None, :]
    factor = jnp.where(coarse_mask, 4.0, 1.0).astype(jnp.float32)
    spread = 1.0 / math.sqrt(TILE * N_COL * TPD / RB)
    return (entries * factor * spread).astype(jnp.bfloat16)


def draw_tile_count(key, part):
    first_key = jax.random.fold_in(key, 21)
    second_key = jax.random.fold_in(key, 22)
    third_key = jax.random.fold_in(key, 23)
    first_draw = jax.random.randint(first_key, (N_ROW * N_COL,), 1, TPD + 1)
    second_draw = jax.random.randint(second_key, (N_ROW * N_COL,), 1, TPD + 1)
    lesser = jnp.minimum(first_draw, second_draw)
    chosen = jax.random.randint(third_key, (), 0, N_ROW * N_COL)
    filled = jnp.where(jnp.arange(N_ROW * N_COL) == chosen, TPD, lesser)
    return filled.reshape(N_ROW, N_COL).astype(jnp.int32)


def touch_ends(values, rng, smallest, high):
    spot = [jax.random.randint(jax.random.fold_in(rng, axis), (), 0, length) for axis, length in enumerate(values.shape)]
    widest = values.shape.index(max(values.shape))
    next_to = spot[:widest] + [(spot[widest] + 1) % values.shape[widest]] + spot[widest + 1:]
    return values.at[tuple(spot)].set(smallest).at[tuple(next_to)].set(high)


def shard_levels(stream_key, dims, shards, low, top_value):
    factor_of, own = 1.0, jax.random.fold_in(stream_key, 6)
    for dim, parts in shards:
        steps = jnp.exp(jax.random.uniform(jax.random.fold_in(own, dim), (parts,), jnp.float32, low / len(shards), top_value / len(shards)))
        factor_of = factor_of * jnp.repeat(steps, dims[dim] // parts).reshape([-1 if axis == dim else 1 for axis in range(len(dims))])
    return factor_of


def normal_values(own_key, dims, width, reach, shards=(), kind=jnp.bfloat16):
    array = jax.random.normal(own_key, dims, jnp.float32) * width
    if len(shards) > 0:
        array = shard_levels(own_key, dims, shards, -0.22, 0.18) * array
    return jnp.clip(array, min=-reach, max=reach).astype(kind)


def setup_inputs(seed: int = 0) -> dict:
    key_list = jax.random.split(jax.random.key(seed), 6)
    sources = normal_values(key_list[0], (R, NP), 1.0, 6.0, ((0, 8), (1, 32)), jnp.float32)
    tiles = draw_tiles(jax.random.fold_in(key_list[5], 71), 0)
    tile_row = touch_ends(jax.random.randint(key_list[2], (N_ROW, N_COL, TPD), 0, RB), jax.random.fold_in(key_list[2], 1), 0, RB - 1).astype(jnp.int32)
    tile_col = touch_ends(jax.random.randint(key_list[3], (N_ROW, N_COL, TPD), 0, CB), jax.random.fold_in(key_list[3], 1), 0, CB - 1).astype(jnp.int32)
    tile_count = draw_tile_count(jax.random.fold_in(key_list[5], 71), 0)
    return {"sources": sources, "tiles": tiles, "tile_row": tile_row, "tile_col": tile_col, "tile_count": tile_count}


ROOT_HALF = 1.0 / math.sqrt(2.0)

def haar_table(extent):
    matrix = np.eye(extent)
    stride = 1
    while stride < extent:
        for position in range(0, extent, 2 * stride):
            first_row = matrix[position].copy()
            second_row = matrix[position + stride].copy()
            matrix[position] = (first_row + second_row) * ROOT_HALF
            matrix[position + stride] = (first_row - second_row) * ROOT_HALF
        stride = stride * 2
    return matrix

def pair_step(values, stride):
    height, extent = values.shape
    shaped = values.reshape(height, extent // (2 * stride), 2, stride)
    first_part = shaped[:, :, 0, 0]
    second_part = shaped[:, :, 1, 0]
    shaped = shaped.at[:, :, 0, 0].set((first_part + second_part) * ROOT_HALF)
    shaped = shaped.at[:, :, 1, 0].set((first_part - second_part) * ROOT_HALF)
    return shaped.reshape(height, extent)

def haar_forward(values):
    stride = 1
    while stride < values.shape[1]:
        values = pair_step(values, stride)
        stride = stride * 2
    return values

def haar_inverse(values):
    stride = values.shape[1] // 2
    while stride >= 1:
        values = pair_step(values, stride)
        stride = stride // 2
    return values

def reference(sources, tiles, tile_row, tile_col, tile_count):
    haar_matrix = jnp.asarray(haar_table(TILE), jnp.float32)
    shaped = sources.reshape(R, NB, TILE)
    local_coef = jnp.einsum('rbk,nk->rbn', shaped, haar_matrix, precision=lax.Precision.HIGHEST)
    scaling = haar_forward(local_coef[:, :, 0])
    wavelet = local_coef.at[:, :, 0].set(scaling).astype(jnp.bfloat16)
    group_offsets = (jnp.arange(N_COL, dtype=jnp.int32) * CB)[:, None]

    def one_row(carried, inputs):
        row_tiles, row_rows, row_cols, row_counts = inputs
        global_cols = (row_cols + group_offsets).reshape(-1)
        side_blocks = jnp.take(wavelet, global_cols, axis=1).astype(jnp.float32)
        stack = row_tiles.reshape(N_COL * TPD, TILE, TILE).astype(jnp.float32)
        product = jnp.einsum('rtk,tkn->rtn', side_blocks, stack, precision=lax.Precision.HIGHEST)
        usable = (jnp.arange(TPD, dtype=jnp.int32)[None, :] < row_counts[:, None]).reshape(-1)
        select = ((row_rows.reshape(-1)[:, None] == jnp.arange(RB, dtype=jnp.int32)[None, :]) & usable[:, None]).astype(jnp.float32)
        return (carried, jnp.einsum('ti,rtn->rin', select, product, precision=lax.Precision.HIGHEST))
    ignored, stacked = lax.scan(one_row, jnp.zeros((), jnp.float32), (tiles, tile_row, tile_col, tile_count))
    image_coef = jnp.transpose(stacked, (1, 0, 2, 3)).reshape(R, NB, TILE)
    back_scaling = haar_inverse(image_coef[:, :, 0])
    image_coef = image_coef.at[:, :, 0].set(back_scaling)
    result = jnp.einsum('rbn,nk->rbk', image_coef, haar_matrix, precision=lax.Precision.HIGHEST)
    return result.reshape(R, NP)
```

```python
import math

import jax
import jax.numpy as jnp
import numpy as np
from jax import lax
from jax.experimental import pallas as pl
from jax.experimental.pallas import tpu as pltpu
from jax.sharding import PartitionSpec as P

MESH = pl.DeviceIdType.MESH
ROOT_HALF = 1.0 / math.sqrt(2.0)
NX, NY, NZ, NK = 4, 4, 8, 2
NROW, NCOL = NX * NZ, NY * NK
TILE = 256
RHS = 16
RB = 8
SLOTS = 48
HALF = RB // 2
LEVELS = 5


def sign_table(extent):
    signs = np.zeros((extent, extent), np.float32)
    factor = np.zeros((extent,), np.float64)
    signs[0] = 1.0
    factor[0] = extent**-0.5
    for n in range(1, extent):
        low = n & -n
        signs[n, n - low : n] = 1.0
        signs[n, n : n + low] = -1.0
        factor[n] = (2.0 * low) ** -0.5
    return signs, factor.astype(np.float32)


def split_dot(values, matrix):
    m = values.shape[0]
    hi = values.astype(jnp.bfloat16)
    rest = values - hi.astype(jnp.float32)
    mid = rest.astype(jnp.bfloat16)
    low = (rest - mid.astype(jnp.float32)).astype(jnp.bfloat16)
    stacked = jnp.concatenate([hi, mid, low], axis=0)
    out = jnp.dot(stacked, matrix, preferred_element_type=jnp.float32)
    return out[:m] + (out[m : 2 * m] + out[2 * m :])


def kernel(
    src_hbm, tiles_hbm, trow, tcol, tcnt, st_ref, s_ref, fac_ref,
    out_ref,
    src, tiles, wav, xa, xb, run, part, recvk, psum, ysend, yrecv, image,
    fsend, frecv, facc, tsend, trecv, prev, last,
    ld_sem, f_ss, f_rs, a_ss, a_rs, l_sem, b_ss, b_rs, r_ss, r_rs, k_ss, k_rs, y_ss, y_rs, t_ss, t_rs,
):
    r = lax.axis_index("row")
    c = lax.axis_index("col")
    x, z = lax.rem(r, NX), r // NX
    y, k = c // NK, lax.rem(c, NK)
    xs = (xa, xb)

    bar = pltpu.get_barrier_semaphore()

    def signal_row(j, carry):
        pl.semaphore_signal(bar, inc=1, device_id=(lax.rem(r + j, NROW), c), device_id_type=MESH)
        return carry

    lax.fori_loop(1, NROW, signal_row, 0)

    def signal_source(j, carry):
        @pl.when(jnp.logical_not(jnp.logical_and(z == c, j == c)))
        def _():
            pl.semaphore_signal(bar, inc=1, device_id=(c * NX + x, j), device_id_type=MESH)

        return carry

    lax.fori_loop(0, NCOL, signal_source, 0)
    pl.semaphore_signal(bar, inc=1, device_id=(r, y * NK + 1 - k), device_id_type=MESH)
    for d in range(1, NY):
        pl.semaphore_signal(bar, inc=1, device_id=(r, lax.rem(y + d, NY) * NK + k), device_id_type=MESH)

    load_src = pltpu.make_async_copy(src_hbm, src, ld_sem.at[0])
    load_src.start()
    load_tiles = pltpu.make_async_copy(tiles_hbm.at[0, 0], tiles, ld_sem.at[1])
    load_tiles.start()

    count = tcnt[0, 0]

    def chain(t, lasts):
        row = jnp.where(t < count, trow[0, 0, t], -1)
        before = jnp.int32(0)
        new = []
        for i in range(RB):
            hit = row == i
            before = jnp.where(hit, lasts[i], before)
            new.append(jnp.where(hit, t + 1, lasts[i]))
        prev[t] = before
        return tuple(new)

    lasts = lax.fori_loop(0, SLOTS, chain, tuple(jnp.int32(0) for _ in range(RB)))
    for i in range(RB):
        last[i] = lasts[i]
    run[0] = jnp.zeros((NY * RHS, TILE), jnp.float32)

    load_src.wait()
    stacked = jnp.concatenate([src[:, b * TILE : (b + 1) * TILE] for b in range(RB)], axis=0)
    coef = split_dot(stacked, st_ref[...]) * fac_ref[...]
    blocks = [coef[b * RHS : (b + 1) * RHS] for b in range(RB)]
    coarse = [blocks[b][:, :128] for b in range(RB)]
    stride = 1
    while stride < RB:
        for p in range(0, RB, 2 * stride):
            u, v = coarse[p], coarse[p + stride]
            coarse[p], coarse[p + stride] = (u + v) * ROOT_HALF, (u - v) * ROOT_HALF
        stride *= 2
    first = lax.broadcasted_iota(jnp.int32, (RHS, 128), 1) == 0
    for b in range(RB):
        low = jnp.where(first, coarse[b], blocks[b][:, :128])
        wav[b, :, :128] = low.astype(jnp.bfloat16)
        wav[b, :, 128:] = blocks[b][:, 128:].astype(jnp.bfloat16)
    fsend[...] = coarse[0]

    pl.semaphore_wait(bar, jnp.where(z == c, NROW - 1 + NCOL - 1 + NY, NROW - 1 + NCOL + NY))

    def f_copy(level, target):
        return pltpu.make_async_remote_copy(
            src_ref=fsend, dst_ref=frecv.at[r], send_sem=f_ss.at[level], recv_sem=f_rs.at[r],
            device_id=(target, c), device_id_type=MESH,
        )

    targets = [(r // 2 ** (lv + 1)) * 2 ** (lv + 1) + 2**lv for lv in range(LEVELS)] + [r * 0]
    for level in reversed(range(LEVELS + 1)):
        @pl.when(targets[level] != r)
        def _():
            f_copy(level, targets[level]).start()

    def half(ref, h):
        return ref.at[pl.ds(HALF - HALF * h, HALF)]

    def piece(ref, ys, xi, h):
        return ref.at[ys, pl.ds(xi * RB + HALF - HALF * h, HALF)]

    ORDER = (1, 7, 2, 6, 3, 5, 4, 0)

    def stage_a(h):
        for kk in range(NK):
            @pl.when(k == kk)
            def _():
                def send(j, carry):
                    zt = lax.rem(z + j, NZ)
                    copy = pltpu.make_async_remote_copy(
                        src_ref=half(wav, h), dst_ref=piece(xs[kk], y, x, h),
                        send_sem=a_ss.at[h * NZ + j], recv_sem=a_rs.at[(h * NK + kk) * NY + y],
                        device_id=(zt * NX + x, z), device_id_type=MESH,
                    )
                    copy.start()
                    return carry

                @pl.when(z != c)
                def _():
                    send(0, 0)

                @pl.when(z == c)
                def _():
                    pltpu.make_async_copy(half(wav, h), piece(xs[kk], y, x, h), l_sem.at[h]).start()

                for j in (4, 3, 5, 2, 6, 1, 7):
                    send(j, 0)

    def stage_a_done(h):
        for j in range(NZ):
            wait = pltpu.make_async_copy(half(wav, h), half(wav, h), a_ss.at[h * NZ + j])
            if j == 0:
                @pl.when(z != c)
                def _():
                    wait.wait()
            else:
                wait.wait()

    def b_copy(kk, ys, h, d):
        ref = xs[kk]
        i = ((h * NK + kk) * NY + ys) * 2 + d
        to = lax.rem(x + 1 + 2 * d, NX)
        return pltpu.make_async_remote_copy(
            src_ref=piece(ref, ys, x, h), dst_ref=piece(ref, ys, x, h),
            send_sem=b_ss.at[i], recv_sem=b_rs.at[i],
            device_id=(z * NX + to, c), device_id_type=MESH,
        )

    def r_copy(kk, ys, h, d):
        ref = xs[kk]
        i = (h * NK + kk) * NY + ys
        to = lax.rem(x + 1 + 2 * d, NX)
        origin = lax.rem(x + 3 - 2 * d, NX)
        return pltpu.make_async_remote_copy(
            src_ref=piece(ref, ys, origin, h), dst_ref=piece(ref, ys, origin, h),
            send_sem=r_ss.at[i], recv_sem=r_rs.at[i],
            device_id=(z * NX + to, c), device_id_type=MESH,
        )

    def wait_for(ref, sem):
        pltpu.make_async_copy(ref, ref, sem).wait()

    def b_arrived(kk, ys, h, d):
        i = ((h * NK + kk) * NY + ys) * 2 + d
        wait_for(piece(xs[kk], ys, lax.rem(x + 3 - 2 * d, NX), h), b_rs.at[i])

    def r_arrived(kk, ys, h):
        i = (h * NK + kk) * NY + ys
        wait_for(piece(xs[kk], ys, lax.rem(x + 2, NX), h), r_rs.at[i])

    def serve(kk, h):
        for ys in range(NY):
            i = (h * NK + kk) * NY + ys
            mine = piece(xs[kk], ys, x, h)
            local = jnp.logical_and(z == c, c == ys * NK + kk)

            @pl.when(local)
            def _():
                pltpu.make_async_copy(mine, mine, l_sem.at[h]).wait()

            @pl.when(jnp.logical_not(local))
            def _():
                pltpu.make_async_copy(mine, mine, a_rs.at[i]).wait()

            b_copy(kk, ys, h, 0).start()
            b_copy(kk, ys, h, 1).start()

    def relay(kk, h):
        for ys in range(NY):
            d = (ys + h) % 2
            b_arrived(kk, ys, h, d)
            r_copy(kk, ys, h, d).start()

    def finish(kk, h):
        for ys in range(NY):
            d = (ys + h) % 2
            b_arrived(kk, ys, h, 1 - d)
            r_arrived(kk, ys, h)

    def sends_done(kk, h):
        for ys in range(NY):
            b_copy(kk, ys, h, 0).wait_send()
            b_copy(kk, ys, h, 1).wait_send()
            r_copy(kk, ys, h, (ys + h) % 2).wait_send()

    stage_a(0)
    serve(0, 0)

    for level in range(LEVELS + 1):
        size = 2 ** (level + 1) if level < LEVELS else NROW
        mine = (lax.rem(r, size) == 2**level) if level < LEVELS else (r == 0)

        @pl.when(mine)
        def _():
            base = (r // size) * size

            def arrive(j, carry):
                sender = base + j

                @pl.when(sender != r)
                def _():
                    pltpu.make_async_copy(fsend, frecv.at[sender], f_rs.at[sender]).wait()

                @pl.when(sender == r)
                def _():
                    frecv[r] = fsend[...]

                return carry

            lax.fori_loop(0, size, arrive, 0)
            total = jnp.zeros((RHS, 128), jnp.float32)
            for j in range(size):
                value = frecv[base + j]
                total = total - value if level < LEVELS and j >= size // 2 else total + value
            facc[...] = total * (size**-0.5)

    wav[0, :, :128] = jnp.where(first, facc[...], wav[0, :, :128].astype(jnp.float32)).astype(jnp.bfloat16)
    stage_a(1)
    serve(1, 0)
    relay(0, 0)
    serve(0, 1)
    relay(1, 0)
    finish(0, 0)
    serve(1, 1)
    relay(0, 1)
    relay(1, 1)
    finish(0, 1)
    load_tiles.wait()

    def compute(kk, lo, hi):
        ref = xs[kk]

        def step(t, carry):
            side = ref[:, pl.ds(tcol[0, 0, t], 1)].reshape(NY * RHS, TILE)
            product = jnp.dot(side, tiles[t], preferred_element_type=jnp.float32)
            run[t + 1] = run[prev[t]] + product
            return carry

        lax.fori_loop(lo, hi, step, 0, unroll=4)

    k_copy = pltpu.make_async_remote_copy(
        src_ref=part, dst_ref=recvk, send_sem=k_ss.at[0], recv_sem=k_rs.at[0],
        device_id=(r, y * NK + 1 - k), device_id_type=MESH,
    )

    def give(kk):
        @pl.when(k != kk)
        def _():
            for i in range(RB):
                part[i] = run[last[i]]
            k_copy.start()

    def y_copy(d):
        to = lax.rem(y + d, NY)
        return pltpu.make_async_remote_copy(
            src_ref=ysend.at[to], dst_ref=yrecv.at[d], send_sem=y_ss.at[d], recv_sem=y_rs.at[d],
            device_id=(r, to * NK + k), device_id_type=MESH,
        )

    def take(kk):
        @pl.when(k == kk)
        def _():
            k_copy.wait_recv()
            for i in range(RB):
                total = (run[last[i]] + recvk[i]).reshape(NY, RHS, TILE)
                psum[:, i] = total
                ysend[:, i] = total.astype(jnp.bfloat16)
            for d in (2, 1, 3):
                y_copy(d).start()

    compute(0, 0, SLOTS)
    give(0)
    take(0)
    finish(1, 0)
    finish(1, 1)
    compute(1, 0, SLOTS)
    give(1)
    take(1)

    for d in (1, 3, 2):
        y_copy(d).wait_recv()
    for i in range(RB):
        total = psum[y, i]
        for d in range(1, NY):
            total = total + yrecv[d, i].astype(jnp.float32)
        image[i] = total
    tsend[...] = image[0, :, :128]

    def t_copy(slot, j, target):
        return pltpu.make_async_remote_copy(
            src_ref=tsend, dst_ref=trecv.at[slot], send_sem=t_ss.at[j], recv_sem=t_rs.at[slot],
            device_id=(target, c), device_id_type=MESH,
        )

    for level in range(LEVELS + 1):
        size = 2 ** (level + 1) if level < LEVELS else NROW
        mine = (lax.rem(r, size) == 2**level) if level < LEVELS else (r == 0)

        @pl.when(mine)
        def _():
            base = (r // size) * size

            def spread(j, carry):
                t_copy(level, j, base + lax.rem(r - base + j, size)).start()
                return carry

            lax.fori_loop(1, size, spread, 0)

    lane0 = lax.broadcasted_iota(jnp.int32, (RHS, TILE), 1) == 0
    plain = jnp.concatenate([jnp.where(lane0, 0.0, image[i]) for i in range(RB)], axis=0)
    result = split_dot(plain * fac_ref[...], s_ref[...])

    top = jnp.zeros((RHS, 128), jnp.float32)
    for level in range(LEVELS + 1):
        @pl.when(targets[level] != r)
        def _():
            pltpu.make_async_copy(tsend, trecv.at[level], t_rs.at[level]).wait()

        @pl.when(targets[level] == r)
        def _():
            trecv[level] = tsend[...]

    for level in range(LEVELS + 1):
        size = 2 ** (level + 1) if level < LEVELS else NROW
        weight = size**-0.5
        if level < LEVELS:
            weight = jnp.where(lax.rem(r, size) < size // 2, weight, -weight)
        top = top + trecv[level] * weight

    back = [top] + [image[i, :, :128] for i in range(1, RB)]
    stride = RB // 2
    while stride >= 1:
        for p in range(0, RB, 2 * stride):
            u, v = back[p], back[p + stride]
            back[p], back[p + stride] = (u + v) * ROOT_HALF, (u - v) * ROOT_HALF
        stride //= 2
    for b in range(RB):
        level0 = jnp.broadcast_to(back[b][:, :1] * (TILE**-0.5), (RHS, TILE))
        out_ref[:, b * TILE : (b + 1) * TILE] = result[b * RHS : (b + 1) * RHS] + level0

    for level in range(LEVELS + 1):
        @pl.when(targets[level] != r)
        def _():
            f_copy(level, targets[level]).wait_send()
    stage_a_done(0)
    stage_a_done(1)
    for h in range(2):
        for kk in range(NK):
            sends_done(kk, h)
    k_copy.wait_send()
    for d in range(1, NY):
        y_copy(d).wait_send()
    for level in range(LEVELS + 1):
        size = 2 ** (level + 1) if level < LEVELS else NROW
        mine = (lax.rem(r, size) == 2**level) if level < LEVELS else (r == 0)

        @pl.when(mine)
        def _():
            def sent(j, carry):
                pltpu.make_async_copy(tsend, tsend, t_ss.at[j]).wait()
                return carry

            lax.fori_loop(1, size, sent, 0)


def local(sources, tiles, tile_row, tile_col, tile_count):
    table, factor = sign_table(TILE)
    s_mat = jnp.asarray(table, jnp.bfloat16)
    st_mat = jnp.asarray(table.T.copy(), jnp.bfloat16)
    fac = jnp.asarray(factor[None, :], jnp.float32)
    vmem = pl.BlockSpec(memory_space=pltpu.VMEM)
    smem = pl.BlockSpec(memory_space=pltpu.SMEM)
    hbm = pl.BlockSpec(memory_space=pl.ANY)
    f32, b16 = jnp.float32, jnp.bfloat16
    dma = pltpu.SemaphoreType.DMA
    return pl.pallas_call(
        kernel,
        out_shape=jax.ShapeDtypeStruct((RHS, RB * TILE), f32),
        in_specs=[hbm, hbm, smem, smem, smem, vmem, vmem, vmem],
        out_specs=vmem,
        scratch_shapes=[
            pltpu.VMEM((RHS, RB * TILE), f32),
            pltpu.VMEM((SLOTS, TILE, TILE), b16),
            pltpu.VMEM((RB, RHS, TILE), b16),
            pltpu.VMEM((NY, NX * RB, RHS, TILE), b16),
            pltpu.VMEM((NY, NX * RB, RHS, TILE), b16),
            pltpu.VMEM((SLOTS + 1, NY * RHS, TILE), f32),
            pltpu.VMEM((RB, NY * RHS, TILE), f32),
            pltpu.VMEM((RB, NY * RHS, TILE), f32),
            pltpu.VMEM((NY, RB, RHS, TILE), f32),
            pltpu.VMEM((NY, RB, RHS, TILE), b16),
            pltpu.VMEM((NY, RB, RHS, TILE), b16),
            pltpu.VMEM((RB, RHS, TILE), f32),
            pltpu.VMEM((RHS, 128), f32),
            pltpu.VMEM((NROW, RHS, 128), f32),
            pltpu.VMEM((RHS, 128), f32),
            pltpu.VMEM((RHS, 128), f32),
            pltpu.VMEM((LEVELS + 1, RHS, 128), f32),
            pltpu.SMEM((SLOTS,), jnp.int32),
            pltpu.SMEM((RB,), jnp.int32),
            dma((2,)),
            dma((LEVELS + 1,)),
            dma((NROW,)),
            dma((2 * NZ,)),
            dma((2 * NCOL,)),
            dma((2,)),
            dma((4 * NCOL,)),
            dma((4 * NCOL,)),
            dma((2 * NCOL,)),
            dma((2 * NCOL,)),
            dma((1,)),
            dma((1,)),
            dma((NY,)),
            dma((NY,)),
            dma((NROW,)),
            dma((LEVELS + 1,)),
        ],
        compiler_params=pltpu.CompilerParams(
            collective_id=0, has_side_effects=True, vmem_limit_bytes=48 * 2**20
        ),
    )(sources, tiles, tile_row, tile_col, tile_count, st_mat, s_mat, fac)


def solution(mesh):
    return jax.shard_map(
        local,
        mesh=mesh,
        in_specs=(
            P("col", "row"),
            P("row", "col", None, None, None),
            P("row", "col", None),
            P("row", "col", None),
            P("row", "col"),
        ),
        out_specs=P("col", "row"),
        check_vma=False,
    )
```

```python
import math

import jax
import jax.numpy as jnp
import numpy as np
from jax import lax
from jax.experimental import pallas as pl
from jax.experimental.pallas import tpu as pltpu
from jax.sharding import PartitionSpec as P

MESH = pl.DeviceIdType.MESH
ROOT_HALF = 1.0 / math.sqrt(2.0)
NX, NY, NZ, NK = 4, 4, 8, 2
NROW, NCOL = NX * NZ, NY * NK
TILE = 256
RHS = 16
RB = 8
SLOTS = 48
HALF = RB // 2
LEVELS = 5


def sign_table(extent):
    signs = np.zeros((extent, extent), np.float32)
    factor = np.zeros((extent,), np.float64)
    signs[0] = 1.0
    factor[0] = extent**-0.5
    for n in range(1, extent):
        low = n & -n
        signs[n, n - low : n] = 1.0
        signs[n, n : n + low] = -1.0
        factor[n] = (2.0 * low) ** -0.5
    return signs, factor.astype(np.float32)


def split_dot(values, matrix):
    m = values.shape[0]
    hi = values.astype(jnp.bfloat16)
    rest = values - hi.astype(jnp.float32)
    mid = rest.astype(jnp.bfloat16)
    low = (rest - mid.astype(jnp.float32)).astype(jnp.bfloat16)
    stacked = jnp.concatenate([hi, mid, low], axis=0)
    out = jnp.dot(stacked, matrix, preferred_element_type=jnp.float32)
    return out[:m] + (out[m : 2 * m] + out[2 * m :])


def kernel(
    src_hbm, tiles_hbm, trow_hbm, tcol_hbm, tcnt_hbm, st_hbm, s_hbm, fac_hbm,
    out_ref,
    trow, tcol, tcnt, st_ref, s_ref, fac_ref,
    src, tiles, wav, xa, xb, run, part, recvk, psum, ysend, yrecv, image,
    fsend, frecv, facc, tsend, trecv, prev, last,
    ld_sem, f_ss, f_rs, a_ss, a_rs, l_sem, b_ss, b_rs, r_ss, r_rs, k_ss, k_rs, y_ss, y_rs, t_ss, t_rs,
):
    r = lax.axis_index("row")
    c = lax.axis_index("col")
    x, z = lax.rem(r, NX), r // NX
    y, k = c // NK, lax.rem(c, NK)
    xs = (xa, xb)

    bar = pltpu.get_barrier_semaphore()

    def signal_row(j, carry):
        pl.semaphore_signal(bar, inc=1, device_id=(lax.rem(r + j, NROW), c), device_id_type=MESH)
        return carry

    lax.fori_loop(1, NROW, signal_row, 0)

    def signal_source(j, carry):
        @pl.when(jnp.logical_not(jnp.logical_and(z == c, j == c)))
        def _():
            pl.semaphore_signal(bar, inc=1, device_id=(c * NX + x, j), device_id_type=MESH)

        return carry

    lax.fori_loop(0, NCOL, signal_source, 0)
    pl.semaphore_signal(bar, inc=1, device_id=(r, y * NK + 1 - k), device_id_type=MESH)
    for d in range(1, NY):
        pl.semaphore_signal(bar, inc=1, device_id=(r, lax.rem(y + d, NY) * NK + k), device_id_type=MESH)

    pairs = (
        (trow_hbm, trow), (tcol_hbm, tcol), (tcnt_hbm, tcnt), (src_hbm, src), (st_hbm, st_ref), (fac_hbm, fac_ref),
        (s_hbm, s_ref), (tiles_hbm.at[0, 0], tiles),
    )
    loads = [pltpu.make_async_copy(a, b, ld_sem.at[i]) for i, (a, b) in enumerate(pairs)]
    for load in loads:
        load.start()
    for load in loads[:3]:
        load.wait()

    count = tcnt[0, 0]

    def chain(t, lasts):
        row = jnp.where(t < count, trow[0, 0, t], -1)
        before = jnp.int32(0)
        new = []
        for i in range(RB):
            hit = row == i
            before = jnp.where(hit, lasts[i], before)
            new.append(jnp.where(hit, t + 1, lasts[i]))
        prev[t] = before
        return tuple(new)

    lasts = lax.fori_loop(0, SLOTS, chain, tuple(jnp.int32(0) for _ in range(RB)))
    for i in range(RB):
        last[i] = lasts[i]
    run[0] = jnp.zeros((NY * RHS, TILE), jnp.float32)

    for load in loads[3:6]:
        load.wait()
    stacked = jnp.concatenate([src[:, b * TILE : (b + 1) * TILE] for b in range(RB)], axis=0)
    coef = split_dot(stacked, st_ref[...]) * fac_ref[...]
    blocks = [coef[b * RHS : (b + 1) * RHS] for b in range(RB)]
    coarse = [blocks[b][:, :128] for b in range(RB)]
    stride = 1
    while stride < RB:
        for p in range(0, RB, 2 * stride):
            u, v = coarse[p], coarse[p + stride]
            coarse[p], coarse[p + stride] = (u + v) * ROOT_HALF, (u - v) * ROOT_HALF
        stride *= 2
    first = lax.broadcasted_iota(jnp.int32, (RHS, 128), 1) == 0
    for b in range(RB):
        low = jnp.where(first, coarse[b], blocks[b][:, :128])
        wav[b, :, :128] = low.astype(jnp.bfloat16)
        wav[b, :, 128:] = blocks[b][:, 128:].astype(jnp.bfloat16)
    fsend[...] = coarse[0]

    pl.semaphore_wait(bar, jnp.where(z == c, NROW - 1 + NCOL - 1 + NY, NROW - 1 + NCOL + NY))

    def f_copy(level, target):
        return pltpu.make_async_remote_copy(
            src_ref=fsend, dst_ref=frecv.at[r], send_sem=f_ss.at[level], recv_sem=f_rs.at[r],
            device_id=(target, c), device_id_type=MESH,
        )

    targets = [(r // 2 ** (lv + 1)) * 2 ** (lv + 1) + 2**lv for lv in range(LEVELS)] + [r * 0]
    for level in reversed(range(LEVELS + 1)):
        @pl.when(targets[level] != r)
        def _():
            f_copy(level, targets[level]).start()

    def half(ref, h):
        return ref.at[pl.ds(HALF - HALF * h, HALF)]

    def piece(ref, ys, xi, h):
        return ref.at[ys, pl.ds(xi * RB + HALF - HALF * h, HALF)]

    def stage_a(h):
        for kk in range(NK):
            @pl.when(k == kk)
            def _():
                def send(j, carry):
                    dz = lax.rem(NK * y + kk + j, NZ)
                    to = lax.rem(z + dz, NZ)
                    mine = jnp.logical_and(dz == 0, z == c)

                    @pl.when(jnp.logical_not(mine))
                    def _():
                        pltpu.make_async_remote_copy(
                            src_ref=half(wav, h), dst_ref=piece(xs[kk], y, x, h),
                            send_sem=a_ss.at[h * NZ + j], recv_sem=a_rs.at[(h * NK + kk) * NY + y],
                            device_id=(to * NX + x, z), device_id_type=MESH,
                        ).start()

                    @pl.when(mine)
                    def _():
                        pltpu.make_async_copy(half(wav, h), piece(xs[kk], y, x, h), l_sem.at[h]).start()

                    return carry

                lax.fori_loop(0, NZ, send, 0)

    def stage_a_done(h):
        for j in range(NZ):
            @pl.when(jnp.logical_not(jnp.logical_and(lax.rem(NK * y + k + j, NZ) == 0, z == c)))
            def _():
                pltpu.make_async_copy(half(wav, h), half(wav, h), a_ss.at[h * NZ + j]).wait()

    def source(kk, m):
        return lax.rem(lax.rem(z - c + 2 * NZ - kk, NZ) // 2 - m + NY, NY)

    def b_copy(kk, ys, h, d):
        ref = xs[kk]
        i = ((h * NK + kk) * NY + ys) * 2 + d
        to = lax.rem(x + 1 + 2 * d, NX)
        return pltpu.make_async_remote_copy(
            src_ref=piece(ref, ys, x, h), dst_ref=piece(ref, ys, x, h),
            send_sem=b_ss.at[i], recv_sem=b_rs.at[i],
            device_id=(z * NX + to, c), device_id_type=MESH,
        )

    def r_copy(kk, ys, h, d):
        ref = xs[kk]
        i = (h * NK + kk) * NY + ys
        to = lax.rem(x + 1 + 2 * d, NX)
        origin = lax.rem(x + 3 - 2 * d, NX)
        return pltpu.make_async_remote_copy(
            src_ref=piece(ref, ys, origin, h), dst_ref=piece(ref, ys, origin, h),
            send_sem=r_ss.at[i], recv_sem=r_rs.at[i],
            device_id=(z * NX + to, c), device_id_type=MESH,
        )

    def wait_for(ref, sem):
        pltpu.make_async_copy(ref, ref, sem).wait()

    def b_arrived(kk, ys, h, d):
        i = ((h * NK + kk) * NY + ys) * 2 + d
        wait_for(piece(xs[kk], ys, lax.rem(x + 3 - 2 * d, NX), h), b_rs.at[i])

    def r_arrived(kk, ys, h):
        i = (h * NK + kk) * NY + ys
        wait_for(piece(xs[kk], ys, lax.rem(x + 2, NX), h), r_rs.at[i])

    def serve(kk, h, m):
        ys = source(kk, m)
        i = (h * NK + kk) * NY + ys
        mine = piece(xs[kk], ys, x, h)
        local = jnp.logical_and(z == c, c == ys * NK + kk)

        @pl.when(local)
        def _():
            wait_for(mine, l_sem.at[h])

        @pl.when(jnp.logical_not(local))
        def _():
            wait_for(mine, a_rs.at[i])

        b_copy(kk, ys, h, 0).start()
        b_copy(kk, ys, h, 1).start()

    def relay(kk, h, m):
        ys = source(kk, m)
        d = (m + h) % 2
        b_arrived(kk, ys, h, d)
        r_copy(kk, ys, h, d).start()

    def finish(kk, h):
        for m in range(NY):
            ys = source(kk, m)
            b_arrived(kk, ys, h, 1 - (m + h) % 2)
            r_arrived(kk, ys, h)

    def sends_done(kk, h):
        for m in range(NY):
            ys = source(kk, m)
            b_copy(kk, ys, h, 0).wait_send()
            b_copy(kk, ys, h, 1).wait_send()
            r_copy(kk, ys, h, (m + h) % 2).wait_send()

    stage_a(0)
    for m in range(2):
        serve(0, 0, m)
        serve(1, 0, m)

    for level in range(LEVELS + 1):
        size = 2 ** (level + 1) if level < LEVELS else NROW
        mine = (lax.rem(r, size) == 2**level) if level < LEVELS else (r == 0)

        @pl.when(mine)
        def _():
            base = (r // size) * size

            def arrive(j, carry):
                sender = base + j

                @pl.when(sender != r)
                def _():
                    pltpu.make_async_copy(fsend, frecv.at[sender], f_rs.at[sender]).wait()

                @pl.when(sender == r)
                def _():
                    frecv[r] = fsend[...]

                return carry

            lax.fori_loop(0, size, arrive, 0)
            total = jnp.zeros((RHS, 128), jnp.float32)
            for j in range(size):
                value = frecv[base + j]
                total = total - value if level < LEVELS and j >= size // 2 else total + value
            facc[...] = total * (size**-0.5)

    wav[0, :, :128] = jnp.where(first, facc[...], wav[0, :, :128].astype(jnp.float32)).astype(jnp.bfloat16)
    @pl.when(k == 0)
    def _():
        stage_a(1)

    for m in range(2, NY):
        serve(0, 0, m)
        relay(0, 0, m - 2)
        serve(1, 0, m)
        relay(1, 0, m - 2)

    @pl.when(k == 1)
    def _():
        stage_a(1)

    for m in range(NY):
        serve(0, 1, m)
        if m < 2:
            relay(0, 0, m + 2)
            relay(1, 0, m + 2)
        else:
            relay(0, 1, m - 2)
    for m in range(NY):
        serve(1, 1, m)
        if m < 2:
            relay(0, 1, m + 2)
        else:
            relay(1, 1, m - 2)
    relay(1, 1, 2)
    relay(1, 1, 3)
    finish(0, 0)
    finish(0, 1)
    loads[6].wait()
    loads[7].wait()

    def compute(kk, lo, hi):
        ref = xs[kk]

        def step(t, carry):
            side = ref[:, pl.ds(tcol[0, 0, t], 1)].reshape(NY * RHS, TILE)
            product = jnp.dot(side, tiles[t], preferred_element_type=jnp.float32)
            run[t + 1] = run[prev[t]] + product
            return carry

        lax.fori_loop(lo, hi, step, 0, unroll=4)

    k_copy = pltpu.make_async_remote_copy(
        src_ref=part, dst_ref=recvk, send_sem=k_ss.at[0], recv_sem=k_rs.at[0],
        device_id=(r, y * NK + 1 - k), device_id_type=MESH,
    )

    def give(kk):
        @pl.when(k != kk)
        def _():
            for i in range(RB):
                part[i] = run[last[i]]
            k_copy.start()

    def y_copy(d):
        to = lax.rem(y + d, NY)
        return pltpu.make_async_remote_copy(
            src_ref=ysend.at[to], dst_ref=yrecv.at[d], send_sem=y_ss.at[d], recv_sem=y_rs.at[d],
            device_id=(r, to * NK + k), device_id_type=MESH,
        )

    def take(kk):
        @pl.when(k == kk)
        def _():
            k_copy.wait_recv()
            for i in range(RB):
                total = (run[last[i]] + recvk[i]).reshape(NY, RHS, TILE)
                psum[:, i] = total
                ysend[:, i] = total.astype(jnp.bfloat16)
            for d in (2, 1, 3):
                y_copy(d).start()

    compute(0, 0, SLOTS)
    give(0)
    take(0)
    finish(1, 0)
    finish(1, 1)
    compute(1, 0, SLOTS)
    give(1)
    take(1)

    for d in (1, 3, 2):
        y_copy(d).wait_recv()
    for i in range(RB):
        total = psum[y, i]
        for d in range(1, NY):
            total = total + yrecv[d, i].astype(jnp.float32)
        image[i] = total
    tsend[...] = image[0, :, :128]

    def t_copy(slot, j, target):
        return pltpu.make_async_remote_copy(
            src_ref=tsend, dst_ref=trecv.at[slot], send_sem=t_ss.at[j], recv_sem=t_rs.at[slot],
            device_id=(target, c), device_id_type=MESH,
        )

    for level in range(LEVELS + 1):
        size = 2 ** (level + 1) if level < LEVELS else NROW
        mine = (lax.rem(r, size) == 2**level) if level < LEVELS else (r == 0)

        @pl.when(mine)
        def _():
            base = (r // size) * size

            def spread(j, carry):
                t_copy(level, j, base + lax.rem(r - base + j, size)).start()
                return carry

            lax.fori_loop(1, size, spread, 0)

    lane0 = lax.broadcasted_iota(jnp.int32, (RHS, TILE), 1) == 0
    plain = jnp.concatenate([jnp.where(lane0, 0.0, image[i]) for i in range(RB)], axis=0)
    result = split_dot(plain * fac_ref[...], s_ref[...])

    top = jnp.zeros((RHS, 128), jnp.float32)
    for level in range(LEVELS + 1):
        @pl.when(targets[level] != r)
        def _():
            pltpu.make_async_copy(tsend, trecv.at[level], t_rs.at[level]).wait()

        @pl.when(targets[level] == r)
        def _():
            trecv[level] = tsend[...]

    for level in range(LEVELS + 1):
        size = 2 ** (level + 1) if level < LEVELS else NROW
        weight = size**-0.5
        if level < LEVELS:
            weight = jnp.where(lax.rem(r, size) < size // 2, weight, -weight)
        top = top + trecv[level] * weight

    back = [top] + [image[i, :, :128] for i in range(1, RB)]
    stride = RB // 2
    while stride >= 1:
        for p in range(0, RB, 2 * stride):
            u, v = back[p], back[p + stride]
            back[p], back[p + stride] = (u + v) * ROOT_HALF, (u - v) * ROOT_HALF
        stride //= 2
    for b in range(RB):
        level0 = jnp.broadcast_to(back[b][:, :1] * (TILE**-0.5), (RHS, TILE))
        out_ref[:, b * TILE : (b + 1) * TILE] = result[b * RHS : (b + 1) * RHS] + level0

    for level in range(LEVELS + 1):
        @pl.when(targets[level] != r)
        def _():
            f_copy(level, targets[level]).wait_send()
    stage_a_done(0)
    stage_a_done(1)
    for h in range(2):
        for kk in range(NK):
            sends_done(kk, h)
    k_copy.wait_send()
    for d in range(1, NY):
        y_copy(d).wait_send()
    for level in range(LEVELS + 1):
        size = 2 ** (level + 1) if level < LEVELS else NROW
        mine = (lax.rem(r, size) == 2**level) if level < LEVELS else (r == 0)

        @pl.when(mine)
        def _():
            def sent(j, carry):
                pltpu.make_async_copy(tsend, tsend, t_ss.at[j]).wait()
                return carry

            lax.fori_loop(1, size, sent, 0)


def local(sources, tiles, tile_row, tile_col, tile_count):
    table, factor = sign_table(TILE)
    s_mat = jnp.asarray(table, jnp.bfloat16)
    st_mat = jnp.asarray(table.T.copy(), jnp.bfloat16)
    fac = jnp.asarray(factor[None, :], jnp.float32)
    vmem = pl.BlockSpec(memory_space=pltpu.VMEM)
    hbm = pl.BlockSpec(memory_space=pltpu.HBM)
    f32, b16 = jnp.float32, jnp.bfloat16
    dma = pltpu.SemaphoreType.DMA
    return pl.pallas_call(
        kernel,
        out_shape=jax.ShapeDtypeStruct((RHS, RB * TILE), f32),
        in_specs=[hbm] * 8,
        out_specs=vmem,
        scratch_shapes=[
            pltpu.SMEM((1, 1, SLOTS), jnp.int32),
            pltpu.SMEM((1, 1, SLOTS), jnp.int32),
            pltpu.SMEM((1, 1), jnp.int32),
            pltpu.VMEM((TILE, TILE), b16),
            pltpu.VMEM((TILE, TILE), b16),
            pltpu.VMEM((1, TILE), f32),
            pltpu.VMEM((RHS, RB * TILE), f32),
            pltpu.VMEM((SLOTS, TILE, TILE), b16),
            pltpu.VMEM((RB, RHS, TILE), b16),
            pltpu.VMEM((NY, NX * RB, RHS, TILE), b16),
            pltpu.VMEM((NY, NX * RB, RHS, TILE), b16),
            pltpu.VMEM((SLOTS + 1, NY * RHS, TILE), f32),
            pltpu.VMEM((RB, NY * RHS, TILE), f32),
            pltpu.VMEM((RB, NY * RHS, TILE), f32),
            pltpu.VMEM((NY, RB, RHS, TILE), f32),
            pltpu.VMEM((NY, RB, RHS, TILE), b16),
            pltpu.VMEM((NY, RB, RHS, TILE), b16),
            pltpu.VMEM((RB, RHS, TILE), f32),
            pltpu.VMEM((RHS, 128), f32),
            pltpu.VMEM((NROW, RHS, 128), f32),
            pltpu.VMEM((RHS, 128), f32),
            pltpu.VMEM((RHS, 128), f32),
            pltpu.VMEM((LEVELS + 1, RHS, 128), f32),
            pltpu.SMEM((SLOTS,), jnp.int32),
            pltpu.SMEM((RB,), jnp.int32),
            dma((8,)),
            dma((LEVELS + 1,)),
            dma((NROW,)),
            dma((2 * NZ,)),
            dma((2 * NCOL,)),
            dma((2,)),
            dma((4 * NCOL,)),
            dma((4 * NCOL,)),
            dma((2 * NCOL,)),
            dma((2 * NCOL,)),
            dma((1,)),
            dma((1,)),
            dma((NY,)),
            dma((NY,)),
            dma((NROW,)),
            dma((LEVELS + 1,)),
        ],
        compiler_params=pltpu.CompilerParams(
            collective_id=0, has_side_effects=True, vmem_limit_bytes=64 * 2**20
        ),
    )(sources, tiles, tile_row, tile_col, tile_count, st_mat, s_mat, fac)


def solution(mesh):
    return jax.shard_map(
        local,
        mesh=mesh,
        in_specs=(
            P("col", "row"),
            P("row", "col", None, None, None),
            P("row", "col", None),
            P("row", "col", None),
            P("row", "col"),
        ),
        out_specs=P("col", "row"),
        check_vma=False,
    )
```

```python
import math

import jax
import jax.numpy as jnp
import numpy as np
from jax import lax
from jax.experimental import pallas as pl
from jax.experimental.pallas import tpu as pltpu
from jax.sharding import PartitionSpec as P

MESH = pl.DeviceIdType.MESH
ROOT_HALF = 1.0 / math.sqrt(2.0)
NX, NY, NZ, NK = 4, 4, 8, 2
NROW, NCOL = NX * NZ, NY * NK
TILE = 256
RHS = 16
RB = 8
SLOTS = 48
PARTS = ((4, 4), (0, 4))
NPART = len(PARTS)
LAG = 8
BEFORE = 2
MIDDLE = 6


def direct(m, h):
    return h == NPART - 1 and m >= NCOL - 1


LEVELS = 5


def sign_table(extent):
    signs = np.zeros((extent, extent), np.float32)
    factor = np.zeros((extent,), np.float64)
    signs[0] = 1.0
    factor[0] = extent**-0.5
    for n in range(1, extent):
        low = n & -n
        signs[n, n - low : n] = 1.0
        signs[n, n : n + low] = -1.0
        factor[n] = (2.0 * low) ** -0.5
    return signs, factor.astype(np.float32)


def split_dot(values, matrix):
    m = values.shape[0]
    hi = values.astype(jnp.bfloat16)
    rest = values - hi.astype(jnp.float32)
    mid = rest.astype(jnp.bfloat16)
    low = (rest - mid.astype(jnp.float32)).astype(jnp.bfloat16)
    stacked = jnp.concatenate([hi, mid, low], axis=0)
    out = jnp.dot(stacked, matrix, preferred_element_type=jnp.float32)
    return out[:m] + (out[m : 2 * m] + out[2 * m :])


def kernel(
    src_hbm, tiles_hbm, trow_hbm, tcol_hbm, tcnt_hbm, st_hbm, s_hbm, fac_hbm,
    out_ref,
    trow, tcol, tcnt, trow_v, tcol_v, st_ref, s_ref, fac_ref,
    src, tiles, wav, xa, run, part, recvk, ysend, yrecv, image,
    fsend, frecv, facc, tsend, trecv, column, upart, urecv, prev, last,
    ld_sem, f_ss, f_rs, a_ss, a_rs, l_sem, b_ss, b_rs, r_ss, r_rs, k_ss, k_rs, y_ss, y_rs, t_ss, t_rs, u_ss, u_rs,
):
    r = lax.axis_index("row")
    c = lax.axis_index("col")
    x, z = lax.rem(r, NX), r // NX
    y, k = c // NK, lax.rem(c, NK)

    bar = pltpu.get_barrier_semaphore()

    def signal_row(j, carry):
        pl.semaphore_signal(bar, inc=1, device_id=(lax.rem(r + j, NROW), c), device_id_type=MESH)
        return carry

    lax.fori_loop(1, NROW, signal_row, 0)

    def signal_source(j, carry):
        @pl.when(jnp.logical_not(jnp.logical_and(z == c, j == c)))
        def _():
            pl.semaphore_signal(bar, inc=1, device_id=(c * NX + x, j), device_id_type=MESH)

        return carry

    lax.fori_loop(0, NCOL, signal_source, 0)
    for d in range(1, NCOL):
        pl.semaphore_signal(bar, inc=1, device_id=(r, lax.rem(c + d, NCOL)), device_id_type=MESH)

    pairs = (
        (trow_hbm, trow), (tcol_hbm, tcol), (tcnt_hbm, tcnt), (src_hbm, src), (st_hbm, st_ref), (fac_hbm, fac_ref),
        (s_hbm, s_ref), (tiles_hbm.at[0, 0], tiles), (trow_hbm, trow_v), (tcol_hbm, tcol_v),
    )
    loads = [pltpu.make_async_copy(a, b, ld_sem.at[i]) for i, (a, b) in enumerate(pairs)]
    for load in loads:
        load.start()
    for load in loads[:3]:
        load.wait()

    count = tcnt[0, 0]

    def chain(t, lasts):
        row = jnp.where(t < count, trow[0, 0, t], -1)
        before = jnp.int32(0)
        new = []
        for i in range(RB):
            hit = row == i
            before = jnp.where(hit, lasts[i], before)
            new.append(jnp.where(hit, t + 1, lasts[i]))
        prev[t] = before
        return tuple(new)

    lasts = lax.fori_loop(0, SLOTS, chain, tuple(jnp.int32(0) for _ in range(RB)))
    for i in range(RB):
        last[i] = lasts[i]
    run[0] = jnp.zeros((NCOL, RHS, TILE), jnp.float32)

    for load in loads[3:6]:
        load.wait()
    stacked = jnp.concatenate([src[:, b * TILE : (b + 1) * TILE] for b in range(RB)], axis=0)
    coef = split_dot(stacked, st_ref[...]) * fac_ref[...]
    blocks = [coef[b * RHS : (b + 1) * RHS] for b in range(RB)]
    coarse = [blocks[b][:, :128] for b in range(RB)]
    stride = 1
    while stride < RB:
        for p in range(0, RB, 2 * stride):
            u, v = coarse[p], coarse[p + stride]
            coarse[p], coarse[p + stride] = (u + v) * ROOT_HALF, (u - v) * ROOT_HALF
        stride *= 2
    first = lax.broadcasted_iota(jnp.int32, (RHS, 128), 1) == 0
    for b in range(RB):
        low = jnp.where(first, coarse[b], blocks[b][:, :128])
        wav[b, :, :128] = low.astype(jnp.bfloat16)
        wav[b, :, 128:] = blocks[b][:, 128:].astype(jnp.bfloat16)
    fsend[...] = coarse[0]

    pl.semaphore_wait(bar, NROW - 1 + NCOL - 1 + NCOL - jnp.where(z == c, 1, 0))

    def f_copy(level, target):
        return pltpu.make_async_remote_copy(
            src_ref=fsend, dst_ref=frecv.at[r], send_sem=f_ss.at[level], recv_sem=f_rs.at[r],
            device_id=(target, c), device_id_type=MESH,
        )

    targets = [(r // 2 ** (lv + 1)) * 2 ** (lv + 1) + 2**lv for lv in range(LEVELS)] + [r * 0]
    for level in reversed(range(LEVELS + 1)):
        @pl.when(targets[level] != r)
        def _():
            f_copy(level, targets[level]).start()

    def half(ref, h):
        return ref.at[pl.ds(PARTS[h][0], PARTS[h][1])]

    def piece(cs, xi, h):
        return xa.at[cs, pl.ds(xi * RB + PARTS[h][0], PARTS[h][1])]

    def wait_for(ref, sem):
        pltpu.make_async_copy(ref, ref, sem).wait()

    def stage_a(h):
        def send(j, carry):
            dz = lax.rem(c + j, NZ)
            to = lax.rem(z + dz, NZ)
            mine = jnp.logical_and(dz == 0, z == c)

            @pl.when(jnp.logical_not(mine))
            def _():
                pltpu.make_async_remote_copy(
                    src_ref=half(wav, h), dst_ref=piece(c, x, h),
                    send_sem=a_ss.at[h * NZ + j], recv_sem=a_rs.at[h * NCOL + c],
                    device_id=(to * NX + x, z), device_id_type=MESH,
                ).start()

            @pl.when(mine)
            def _():
                pltpu.make_async_copy(half(wav, h), piece(c, x, h), l_sem.at[h]).start()

            return carry

        lax.fori_loop(0, NZ, send, 0)

    def stage_a_done(h):
        for j in range(NZ):
            @pl.when(jnp.logical_not(jnp.logical_and(lax.rem(c + j, NZ) == 0, z == c)))
            def _():
                wait_for(half(wav, h), a_ss.at[h * NZ + j])

    def source(m):
        return lax.rem(z - c - m + 3 * NZ, NCOL)

    def b_copy(m, h, d):
        cs = source(m)
        i = (h * NCOL + cs) * 2 + d
        to = lax.rem(x + 1 + 2 * d, NX)
        return pltpu.make_async_remote_copy(
            src_ref=piece(cs, x, h), dst_ref=piece(cs, x, h), send_sem=b_ss.at[i], recv_sem=b_rs.at[i],
            device_id=(z * NX + to, c), device_id_type=MESH,
        )

    def r_copy(m, h):
        cs = source(m)
        i = h * NCOL + cs
        d = (m + h) % 2
        if direct(m, h):
            origin, to = x, lax.rem(x + 2, NX)
        else:
            origin, to = lax.rem(x + 3 - 2 * d, NX), lax.rem(x + 1 + 2 * d, NX)
        return pltpu.make_async_remote_copy(
            src_ref=piece(cs, origin, h), dst_ref=piece(cs, origin, h), send_sem=r_ss.at[i], recv_sem=r_rs.at[i],
            device_id=(z * NX + to, c), device_id_type=MESH,
        )

    def b_arrived(m, h, d):
        cs = source(m)
        wait_for(piece(cs, lax.rem(x + 3 - 2 * d, NX), h), b_rs.at[(h * NCOL + cs) * 2 + d])

    def serve(m, h):
        cs = source(m)
        local = jnp.logical_and(z == c, c == cs)

        @pl.when(local)
        def _():
            wait_for(piece(cs, x, h), l_sem.at[h])

        @pl.when(jnp.logical_not(local))
        def _():
            wait_for(piece(cs, x, h), a_rs.at[h * NCOL + cs])

        b_copy(m, h, 0).start()
        b_copy(m, h, 1).start()
        if direct(m, h):
            r_copy(m, h).start()

    def relay(m, h):
        if not direct(m, h):
            b_arrived(m, h, (m + h) % 2)
            r_copy(m, h).start()

    def finish(m, h):
        cs = source(m)
        if direct(m, h):
            b_arrived(m, h, (m + h) % 2)
        b_arrived(m, h, 1 - (m + h) % 2)
        wait_for(piece(cs, lax.rem(x + 2, NX), h), r_rs.at[h * NCOL + cs])

    def sends_done(m, h):
        b_copy(m, h, 0).wait_send()
        b_copy(m, h, 1).wait_send()
        r_copy(m, h).wait_send()

    order = [(m, h) for h in range(NPART) for m in range(NCOL)]

    def serve_range(lo, hi):
        for n in range(lo, hi):
            if n < len(order):
                serve(*order[n])
            if 0 <= n - LAG:
                relay(*order[n - LAG])

    for h in range(NPART - 1):
        stage_a(h)
    serve_range(0, BEFORE)

    for level in range(LEVELS + 1):
        size = 2 ** (level + 1) if level < LEVELS else NROW
        mine = (lax.rem(r, size) == 2**level) if level < LEVELS else (r == 0)

        @pl.when(mine)
        def _():
            base = (r // size) * size

            def arrive(j, carry):
                sender = base + j

                @pl.when(sender != r)
                def _():
                    pltpu.make_async_copy(fsend, frecv.at[sender], f_rs.at[sender]).wait()

                @pl.when(sender == r)
                def _():
                    frecv[r] = fsend[...]

                return carry

            lax.fori_loop(0, size, arrive, 0)
            total = jnp.zeros((RHS, 128), jnp.float32)
            for j in range(size):
                value = frecv[base + j]
                total = total - value if level < LEVELS and j >= size // 2 else total + value
            facc[...] = total * (size**-0.5)

    wav[0, :, :128] = jnp.where(first, facc[...], wav[0, :, :128].astype(jnp.float32)).astype(jnp.bfloat16)
    stage_a(NPART - 1)
    serve_range(BEFORE, MIDDLE)

    for load in loads[6:]:
        load.wait()
    slot_lane = lax.broadcasted_iota(jnp.int32, (TILE, 128), 1)

    def pick(t, found):
        value = tiles[t, :, :128].astype(jnp.float32)
        return jnp.where(slot_lane == t, jnp.broadcast_to(value[:, :1], (TILE, 128)), found)

    found = lax.fori_loop(0, SLOTS, pick, jnp.zeros((TILE, 128), jnp.float32))
    slot = lax.broadcasted_iota(jnp.int32, (NX * RB, SLOTS), 1)
    block = lax.broadcasted_iota(jnp.int32, (NX * RB, SLOTS), 0)
    hit = (tcol_v[0] == block) & (trow_v[0] == 0) & (slot < count)
    column[...] = lax.dot_general(
        hit.astype(jnp.bfloat16), found[:, :SLOTS].astype(jnp.bfloat16), (((1,), (1,)), ((), ())),
        preferred_element_type=jnp.float32,
    )

    serve_range(MIDDLE, len(order) + LAG)
    for m, h in order:
        finish(m, h)

    def compute():
        def step(t, carry):
            side = xa[:, pl.ds(tcol[0, 0, t], 1)].reshape(NCOL * RHS, TILE)
            product = jnp.dot(side, tiles[t], preferred_element_type=jnp.float32)
            run[t + 1] = run[prev[t]] + product.reshape(NCOL, RHS, TILE)
            return carry

        lax.fori_loop(0, SLOTS, step, 0, unroll=16)

    def k_copy(d):
        return pltpu.make_async_remote_copy(
            src_ref=part.at[d], dst_ref=recvk.at[d], send_sem=k_ss.at[d], recv_sem=k_rs.at[d],
            device_id=(r, y * NK + 1 - k), device_id_type=MESH,
        )

    def y_copy(d):
        to = lax.rem(y + d, NY)
        return pltpu.make_async_remote_copy(
            src_ref=ysend.at[d], dst_ref=yrecv.at[d], send_sem=y_ss.at[d], recv_sem=y_rs.at[d],
            device_id=(r, to * NK + k), device_id_type=MESH,
        )

    def swap():
        for d in (2, 1, 3, 0):
            for i in range(RB):
                part[d, i] = run[last[i], lax.rem(y + d, NY) * NK + 1 - k]
            k_copy(d).start()

    def share():
        for d in (2, 1, 3, 0):
            k_copy(d).wait_recv()
            for i in range(RB):
                total = run[last[i], lax.rem(y + d, NY) * NK + k] + recvk[d, i]
                if d:
                    ysend[d, i] = total.astype(jnp.bfloat16)
                else:
                    image[i] = total
            if d:
                y_copy(d).start()

    def u_copy(d):
        to = lax.rem(c + d, NCOL)
        return pltpu.make_async_remote_copy(
            src_ref=upart.at[to], dst_ref=urecv.at[c], send_sem=u_ss.at[d], recv_sem=u_rs.at[c],
            device_id=(r, to), device_id_type=MESH,
        )

    def tops():
        def add(b, total):
            side = xa[:, pl.ds(b, 1)].reshape(NCOL * RHS, TILE).astype(jnp.float32)
            return total + side * column[pl.ds(b, 1), :]

        total = lax.fori_loop(0, NX * RB, add, jnp.zeros((NCOL * RHS, TILE), jnp.float32), unroll=4)
        value = jnp.sum(total, axis=1, keepdims=True)
        upart[...] = jnp.broadcast_to(value, (NCOL * RHS, 128)).reshape(NCOL, RHS, 128)
        for d in (4, 5, 3, 6, 2, 7, 1):
            u_copy(d).start()

    def t_copy(slot, j, target):
        return pltpu.make_async_remote_copy(
            src_ref=tsend, dst_ref=trecv.at[slot], send_sem=t_ss.at[j], recv_sem=t_rs.at[slot],
            device_id=(target, c), device_id_type=MESH,
        )

    def spread_tops():
        urecv[c] = upart[c]
        for d in range(1, NCOL):
            sender = lax.rem(c + d, NCOL)
            wait_for(urecv.at[sender], u_rs.at[sender])
        total = urecv[0]
        for sender in range(1, NCOL):
            total = total + urecv[sender]
        tsend[...] = total
        for level in range(LEVELS + 1):
            size = 2 ** (level + 1) if level < LEVELS else NROW
            mine = (lax.rem(r, size) == 2**level) if level < LEVELS else (r == 0)

            @pl.when(mine)
            def _():
                base = (r // size) * size

                def spread(j, carry):
                    t_copy(level, j, base + lax.rem(r - base + j, size)).start()
                    return carry

                lax.fori_loop(1, size, spread, 0)

    tops()
    compute()
    swap()
    share()
    spread_tops()

    for d in (1, 3, 2):
        y_copy(d).wait_recv()
    for i in range(RB):
        total = image[i]
        for d in range(1, NY):
            total = total + yrecv[d, i].astype(jnp.float32)
        image[i] = total

    lane0 = lax.broadcasted_iota(jnp.int32, (RHS, TILE), 1) == 0
    plain = jnp.concatenate([jnp.where(lane0, 0.0, image[i]) for i in range(RB)], axis=0)
    result = split_dot(plain * fac_ref[...], s_ref[...])

    top = jnp.zeros((RHS, 128), jnp.float32)
    for level in range(LEVELS + 1):
        @pl.when(targets[level] != r)
        def _():
            pltpu.make_async_copy(tsend, trecv.at[level], t_rs.at[level]).wait()

        @pl.when(targets[level] == r)
        def _():
            trecv[level] = tsend[...]

    for level in range(LEVELS + 1):
        size = 2 ** (level + 1) if level < LEVELS else NROW
        weight = size**-0.5
        if level < LEVELS:
            weight = jnp.where(lax.rem(r, size) < size // 2, weight, -weight)
        top = top + trecv[level] * weight

    back = [top] + [image[i, :, :128] for i in range(1, RB)]
    stride = RB // 2
    while stride >= 1:
        for p in range(0, RB, 2 * stride):
            u, v = back[p], back[p + stride]
            back[p], back[p + stride] = (u + v) * ROOT_HALF, (u - v) * ROOT_HALF
        stride //= 2
    for b in range(RB):
        level0 = jnp.broadcast_to(back[b][:, :1] * (TILE**-0.5), (RHS, TILE))
        out_ref[:, b * TILE : (b + 1) * TILE] = result[b * RHS : (b + 1) * RHS] + level0

    for level in range(LEVELS + 1):
        @pl.when(targets[level] != r)
        def _():
            f_copy(level, targets[level]).wait_send()
    for h in range(NPART):
        stage_a_done(h)
    for m, h in order:
        sends_done(m, h)
    for d in range(NY):
        k_copy(d).wait_send()
    for d in range(1, NCOL):
        u_copy(d).wait_send()
    for d in range(1, NY):
        y_copy(d).wait_send()
    for level in range(LEVELS + 1):
        size = 2 ** (level + 1) if level < LEVELS else NROW
        mine = (lax.rem(r, size) == 2**level) if level < LEVELS else (r == 0)

        @pl.when(mine)
        def _():
            def sent(j, carry):
                pltpu.make_async_copy(tsend, tsend, t_ss.at[j]).wait()
                return carry

            lax.fori_loop(1, size, sent, 0)


def local(sources, tiles, tile_row, tile_col, tile_count):
    table, factor = sign_table(TILE)
    s_mat = jnp.asarray(table, jnp.bfloat16)
    st_mat = jnp.asarray(table.T.copy(), jnp.bfloat16)
    fac = jnp.asarray(factor[None, :], jnp.float32)
    vmem = pl.BlockSpec(memory_space=pltpu.VMEM)
    hbm = pl.BlockSpec(memory_space=pltpu.HBM)
    f32, b16 = jnp.float32, jnp.bfloat16
    dma = pltpu.SemaphoreType.DMA
    return pl.pallas_call(
        kernel,
        out_shape=jax.ShapeDtypeStruct((RHS, RB * TILE), f32),
        in_specs=[hbm] * 8,
        out_specs=vmem,
        scratch_shapes=[
            pltpu.SMEM((1, 1, SLOTS), jnp.int32),
            pltpu.SMEM((1, 1, SLOTS), jnp.int32),
            pltpu.SMEM((1, 1), jnp.int32),
            pltpu.VMEM((1, 1, SLOTS), jnp.int32),
            pltpu.VMEM((1, 1, SLOTS), jnp.int32),
            pltpu.VMEM((TILE, TILE), b16),
            pltpu.VMEM((TILE, TILE), b16),
            pltpu.VMEM((1, TILE), f32),
            pltpu.VMEM((RHS, RB * TILE), f32),
            pltpu.VMEM((SLOTS, TILE, TILE), b16),
            pltpu.VMEM((RB, RHS, TILE), b16),
            pltpu.VMEM((NCOL, NX * RB, RHS, TILE), b16),
            pltpu.VMEM((SLOTS + 1, NCOL, RHS, TILE), f32),
            pltpu.VMEM((NY, RB, RHS, TILE), f32),
            pltpu.VMEM((NY, RB, RHS, TILE), f32),
            pltpu.VMEM((NY, RB, RHS, TILE), b16),
            pltpu.VMEM((NY, RB, RHS, TILE), b16),
            pltpu.VMEM((RB, RHS, TILE), f32),
            pltpu.VMEM((RHS, 128), f32),
            pltpu.VMEM((NROW, RHS, 128), f32),
            pltpu.VMEM((RHS, 128), f32),
            pltpu.VMEM((RHS, 128), f32),
            pltpu.VMEM((LEVELS + 1, RHS, 128), f32),
            pltpu.VMEM((NX * RB, TILE), f32),
            pltpu.VMEM((NCOL, RHS, 128), f32),
            pltpu.VMEM((NCOL, RHS, 128), f32),
            pltpu.SMEM((SLOTS,), jnp.int32),
            pltpu.SMEM((RB,), jnp.int32),
            dma((10,)),
            dma((LEVELS + 1,)),
            dma((NROW,)),
            dma((NPART * NZ,)),
            dma((NPART * NCOL,)),
            dma((NPART,)),
            dma((NPART * 2 * NCOL,)),
            dma((NPART * 2 * NCOL,)),
            dma((NPART * NCOL,)),
            dma((NPART * NCOL,)),
            dma((NY,)),
            dma((NY,)),
            dma((NY,)),
            dma((NY,)),
            dma((NROW,)),
            dma((LEVELS + 1,)),
            dma((NCOL,)),
            dma((NCOL,)),
        ],
        compiler_params=pltpu.CompilerParams(
            collective_id=0, has_side_effects=True, vmem_limit_bytes=64 * 2**20
        ),
    )(sources, tiles, tile_row, tile_col, tile_count, st_mat, s_mat, fac)


def solution(mesh):
    return jax.shard_map(
        local,
        mesh=mesh,
        in_specs=(
            P("col", "row"),
            P("row", "col", None, None, None),
            P("row", "col", None),
            P("row", "col", None),
            P("row", "col"),
        ),
        out_specs=P("col", "row"),
        check_vma=False,
    )
```

```python
import math

import jax
import jax.numpy as jnp
import numpy as np
from jax import lax
from jax.experimental import pallas as pl
from jax.experimental.pallas import tpu as pltpu
from jax.sharding import PartitionSpec as P

MESH = pl.DeviceIdType.MESH
ROOT_HALF = 1.0 / math.sqrt(2.0)
NX, NY, NZ, NK = 4, 4, 8, 2
NROW, NCOL = NX * NZ, NY * NK
TILE = 256
RHS = 16
RB = 8
SLOTS = 48
PARTS = ((4, 4), (0, 4))
NPART = len(PARTS)
LAG = 8
BEFORE = 2
MIDDLE = 6
LATER = 13


def direct(m, h):
    return h == NPART - 1 and m >= NCOL - 1


LEVELS = 5


def sign_table(extent):
    signs = np.zeros((extent, extent), np.float32)
    factor = np.zeros((extent,), np.float64)
    signs[0] = 1.0
    factor[0] = extent**-0.5
    for n in range(1, extent):
        low = n & -n
        signs[n, n - low : n] = 1.0
        signs[n, n : n + low] = -1.0
        factor[n] = (2.0 * low) ** -0.5
    return signs, factor.astype(np.float32)


def split_dot(values, matrix):
    m = values.shape[0]
    hi = values.astype(jnp.bfloat16)
    rest = values - hi.astype(jnp.float32)
    mid = rest.astype(jnp.bfloat16)
    low = (rest - mid.astype(jnp.float32)).astype(jnp.bfloat16)
    stacked = jnp.concatenate([hi, mid, low], axis=0)
    out = jnp.dot(stacked, matrix, preferred_element_type=jnp.float32)
    return out[:m] + (out[m : 2 * m] + out[2 * m :])


def kernel(
    src_hbm, tiles_hbm, trow_hbm, tcol_hbm, tcnt_hbm, st_hbm, s_hbm, fac_hbm,
    out_ref,
    trow, tcol, tcnt, trow_v, tcol_v, st_ref, s_ref, fac_ref,
    src, tiles, wav, xa, run, part, recvk, ysend, yrecv, image,
    fsend, frecv, facc, column, erecv, combo, full, upart, prev, last,
    ld_sem, f_ss, f_rs, a_ss, a_rs, l_sem, b_ss, b_rs, r_ss, r_rs, k_ss, k_rs, y_ss, y_rs, e_ss, e_rs,
):
    r = lax.axis_index("row")
    c = lax.axis_index("col")
    x, z = lax.rem(r, NX), r // NX
    y, k = c // NK, lax.rem(c, NK)

    bar = pltpu.get_barrier_semaphore()

    def signal_row(j, carry):
        pl.semaphore_signal(bar, inc=1, device_id=(lax.rem(r + j, NROW), c), device_id_type=MESH)
        return carry

    lax.fori_loop(1, NROW, signal_row, 0)

    def signal_source(j, carry):
        @pl.when(jnp.logical_not(jnp.logical_and(z == c, j == c)))
        def _():
            pl.semaphore_signal(bar, inc=1, device_id=(c * NX + x, j), device_id_type=MESH)

        return carry

    lax.fori_loop(0, NCOL, signal_source, 0)
    pl.semaphore_signal(bar, inc=1, device_id=(r, y * NK + 1 - k), device_id_type=MESH)
    for d in range(1, NY):
        pl.semaphore_signal(bar, inc=1, device_id=(r, lax.rem(y + d, NY) * NK + k), device_id_type=MESH)

    pairs = (
        (trow_hbm, trow), (tcol_hbm, tcol), (tcnt_hbm, tcnt), (src_hbm, src), (st_hbm, st_ref), (fac_hbm, fac_ref),
        (s_hbm, s_ref), (tiles_hbm.at[0, 0], tiles), (trow_hbm, trow_v), (tcol_hbm, tcol_v),
    )
    loads = [pltpu.make_async_copy(a, b, ld_sem.at[i]) for i, (a, b) in enumerate(pairs)]
    for load in loads:
        load.start()
    for load in loads[:3]:
        load.wait()

    count = tcnt[0, 0]

    def chain(t, lasts):
        row = jnp.where(t < count, trow[0, 0, t], -1)
        before = jnp.int32(0)
        new = []
        for i in range(RB):
            hit = row == i
            before = jnp.where(hit, lasts[i], before)
            new.append(jnp.where(hit, t + 1, lasts[i]))
        prev[t] = before
        return tuple(new)

    lasts = lax.fori_loop(0, SLOTS, chain, tuple(jnp.int32(0) for _ in range(RB)))
    for i in range(RB):
        last[i] = lasts[i]
    run[0] = jnp.zeros((NCOL, RHS, TILE), jnp.float32)

    for load in loads[3:6]:
        load.wait()
    stacked = jnp.concatenate([src[:, b * TILE : (b + 1) * TILE] for b in range(RB)], axis=0)
    coef = split_dot(stacked, st_ref[...]) * fac_ref[...]
    blocks = [coef[b * RHS : (b + 1) * RHS] for b in range(RB)]
    coarse = [blocks[b][:, :128] for b in range(RB)]
    stride = 1
    while stride < RB:
        for p in range(0, RB, 2 * stride):
            u, v = coarse[p], coarse[p + stride]
            coarse[p], coarse[p + stride] = (u + v) * ROOT_HALF, (u - v) * ROOT_HALF
        stride *= 2
    first = lax.broadcasted_iota(jnp.int32, (RHS, 128), 1) == 0
    for b in range(RB):
        low = jnp.where(first, coarse[b], blocks[b][:, :128])
        wav[b, :, :128] = low.astype(jnp.bfloat16)
        wav[b, :, 128:] = blocks[b][:, 128:].astype(jnp.bfloat16)
    fsend[...] = coarse[0]

    pl.semaphore_wait(bar, NROW - 1 + NY + NCOL - jnp.where(z == c, 1, 0))

    def f_copy(level, target):
        return pltpu.make_async_remote_copy(
            src_ref=fsend, dst_ref=frecv.at[r], send_sem=f_ss.at[level], recv_sem=f_rs.at[r],
            device_id=(target, c), device_id_type=MESH,
        )

    targets = [(r // 2 ** (lv + 1)) * 2 ** (lv + 1) + 2**lv for lv in range(LEVELS)] + [r * 0]
    for level in reversed(range(LEVELS + 1)):
        @pl.when(targets[level] != r)
        def _():
            f_copy(level, targets[level]).start()

    def half(ref, h):
        return ref.at[pl.ds(PARTS[h][0], PARTS[h][1])]

    def piece(cs, xi, h):
        return xa.at[cs, pl.ds(xi * RB + PARTS[h][0], PARTS[h][1])]

    def wait_for(ref, sem):
        pltpu.make_async_copy(ref, ref, sem).wait()

    def stage_a(h):
        def send(j, carry):
            dz = lax.rem(c + j, NZ)
            to = lax.rem(z + dz, NZ)
            mine = jnp.logical_and(dz == 0, z == c)

            @pl.when(jnp.logical_not(mine))
            def _():
                pltpu.make_async_remote_copy(
                    src_ref=half(wav, h), dst_ref=piece(c, x, h),
                    send_sem=a_ss.at[h * NZ + j], recv_sem=a_rs.at[h * NCOL + c],
                    device_id=(to * NX + x, z), device_id_type=MESH,
                ).start()

            @pl.when(mine)
            def _():
                pltpu.make_async_copy(half(wav, h), piece(c, x, h), l_sem.at[h]).start()

            return carry

        lax.fori_loop(0, NZ, send, 0)

    def stage_a_done(h):
        for j in range(NZ):
            @pl.when(jnp.logical_not(jnp.logical_and(lax.rem(c + j, NZ) == 0, z == c)))
            def _():
                wait_for(half(wav, h), a_ss.at[h * NZ + j])

    def source(m):
        return lax.rem(z - c - m + 3 * NZ, NCOL)

    def b_copy(m, h, d):
        cs = source(m)
        i = (h * NCOL + cs) * 2 + d
        to = lax.rem(x + 1 + 2 * d, NX)
        return pltpu.make_async_remote_copy(
            src_ref=piece(cs, x, h), dst_ref=piece(cs, x, h), send_sem=b_ss.at[i], recv_sem=b_rs.at[i],
            device_id=(z * NX + to, c), device_id_type=MESH,
        )

    def r_copy(m, h):
        cs = source(m)
        i = h * NCOL + cs
        d = (m + h) % 2
        if direct(m, h):
            origin, to = x, lax.rem(x + 2, NX)
        else:
            origin, to = lax.rem(x + 3 - 2 * d, NX), lax.rem(x + 1 + 2 * d, NX)
        return pltpu.make_async_remote_copy(
            src_ref=piece(cs, origin, h), dst_ref=piece(cs, origin, h), send_sem=r_ss.at[i], recv_sem=r_rs.at[i],
            device_id=(z * NX + to, c), device_id_type=MESH,
        )

    def b_arrived(m, h, d):
        cs = source(m)
        wait_for(piece(cs, lax.rem(x + 3 - 2 * d, NX), h), b_rs.at[(h * NCOL + cs) * 2 + d])

    def serve(m, h):
        cs = source(m)
        local = jnp.logical_and(z == c, c == cs)

        @pl.when(local)
        def _():
            wait_for(piece(cs, x, h), l_sem.at[h])

        @pl.when(jnp.logical_not(local))
        def _():
            wait_for(piece(cs, x, h), a_rs.at[h * NCOL + cs])

        b_copy(m, h, 0).start()
        b_copy(m, h, 1).start()
        if direct(m, h):
            r_copy(m, h).start()

    def relay(m, h):
        if not direct(m, h):
            b_arrived(m, h, (m + h) % 2)
            r_copy(m, h).start()

    def finish(m, h):
        cs = source(m)
        if direct(m, h):
            b_arrived(m, h, (m + h) % 2)
        b_arrived(m, h, 1 - (m + h) % 2)
        wait_for(piece(cs, lax.rem(x + 2, NX), h), r_rs.at[h * NCOL + cs])

    def sends_done(m, h):
        b_copy(m, h, 0).wait_send()
        b_copy(m, h, 1).wait_send()
        r_copy(m, h).wait_send()

    order = [(m, h) for h in range(NPART) for m in range(NCOL)]

    def serve_range(lo, hi):
        for n in range(lo, hi):
            if n < len(order):
                serve(*order[n])
            if 0 <= n - LAG:
                relay(*order[n - LAG])

    for h in range(NPART - 1):
        stage_a(h)
    serve_range(0, BEFORE)

    for level in range(LEVELS + 1):
        size = 2 ** (level + 1) if level < LEVELS else NROW
        mine = (lax.rem(r, size) == 2**level) if level < LEVELS else (r == 0)

        @pl.when(mine)
        def _():
            base = (r // size) * size

            def arrive(j, carry):
                sender = base + j

                @pl.when(sender != r)
                def _():
                    pltpu.make_async_copy(fsend, frecv.at[sender], f_rs.at[sender]).wait()

                @pl.when(sender == r)
                def _():
                    frecv[r] = fsend[...]

                return carry

            lax.fori_loop(0, size, arrive, 0)
            total = jnp.zeros((RHS, 128), jnp.float32)
            for j in range(size):
                value = frecv[base + j]
                total = total - value if level < LEVELS and j >= size // 2 else total + value
            facc[...] = total * (size**-0.5)

    wav[0, :, :128] = jnp.where(first, facc[...], wav[0, :, :128].astype(jnp.float32)).astype(jnp.bfloat16)
    stage_a(NPART - 1)
    serve_range(BEFORE, MIDDLE)

    for load in loads[6:]:
        load.wait()
    slot_lane = lax.broadcasted_iota(jnp.int32, (TILE, 128), 1)

    def pick(t, found):
        value = tiles[t, :, :128].astype(jnp.float32)
        return jnp.where(slot_lane == t, jnp.broadcast_to(value[:, :1], (TILE, 128)), found)

    found = lax.fori_loop(0, SLOTS, pick, jnp.zeros((TILE, 128), jnp.float32))
    slot = lax.broadcasted_iota(jnp.int32, (NX * RB, SLOTS), 1)
    block = lax.broadcasted_iota(jnp.int32, (NX * RB, SLOTS), 0)
    hit = (tcol_v[0] == block) & (trow_v[0] == 0) & (slot < count)
    column[...] = lax.dot_general(
        hit.astype(jnp.bfloat16), found[:, :SLOTS].astype(jnp.bfloat16), (((1,), (1,)), ((), ())),
        preferred_element_type=jnp.float32,
    )

    def e_copy(ref, slot, j, target):
        return pltpu.make_async_remote_copy(
            src_ref=ref, dst_ref=erecv.at[slot], send_sem=e_ss.at[j], recv_sem=e_rs.at[slot],
            device_id=(target, c), device_id_type=MESH,
        )

    def owners(act):
        for level in range(LEVELS + 1):
            size = 2 ** (level + 1) if level < LEVELS else NROW
            jump = 1 if level < 2 else NX
            mine = (lax.rem(r, size) == 2**level) if level < LEVELS else (r == 0)

            @pl.when(mine)
            def _():
                def each(j, carry):
                    base = (r // size) * size
                    act(e_copy(column, level, j, base + lax.rem(r - base + j * jump, size)))
                    return carry

                lax.fori_loop(1, size // jump, each, 0)

    def heirs(act):
        for j in range(1, NX):
            act(e_copy(combo, LEVELS + 1, NZ + j, r + j))

    def arrive(levels):
        for level in levels:
            @pl.when(targets[level] != r)
            def _():
                wait_for(erecv.at[level], e_rs.at[level])

            @pl.when(targets[level] == r)
            def _():
                erecv[level] = column[...]

    def weighted(levels):
        total = jnp.zeros((NX * RB, TILE), jnp.float32)
        for level in levels:
            size = 2 ** (level + 1) if level < LEVELS else NROW
            weight = size**-0.5
            if level < LEVELS:
                weight = jnp.where(lax.rem(r, size) < size // 2, weight, -weight)
            total = total + erecv[level] * weight
        return total

    owners(lambda copy: copy.start())
    serve_range(MIDDLE, LATER)

    @pl.when(x == 0)
    def _():
        arrive(range(2, LEVELS + 1))
        combo[...] = weighted(range(2, LEVELS + 1))
        heirs(lambda copy: copy.start())

    serve_range(LATER, len(order) + LAG)

    @pl.when(x != 0)
    def _():
        wait_for(erecv.at[LEVELS + 1], e_rs.at[LEVELS + 1])
        full[...] = erecv[LEVELS + 1]

    @pl.when(x == 0)
    def _():
        full[...] = combo[...]

    arrive(range(2))
    full[...] = full[...] + weighted(range(2))

    for m, h in order:
        finish(m, h)

    def top():
        def add(b, total):
            side = xa[:, pl.ds(b, 1)].reshape(NCOL * RHS, TILE).astype(jnp.float32)
            return total + side * full[pl.ds(b, 1), :]

        total = lax.fori_loop(0, NX * RB, add, jnp.zeros((NCOL * RHS, TILE), jnp.float32), unroll=4)
        value = jnp.sum(total, axis=1, keepdims=True)
        upart[...] = jnp.broadcast_to(value, (NCOL * RHS, 128)).reshape(NCOL, RHS, 128)

    def compute():
        def step(t, carry):
            side = xa[:, pl.ds(tcol[0, 0, t], 1)].reshape(NCOL * RHS, TILE)
            product = jnp.dot(side, tiles[t], preferred_element_type=jnp.float32)
            run[t + 1] = run[prev[t]] + product.reshape(NCOL, RHS, TILE)
            return carry

        lax.fori_loop(0, SLOTS, step, 0, unroll=16)

    def k_copy(d):
        return pltpu.make_async_remote_copy(
            src_ref=part.at[d], dst_ref=recvk.at[d], send_sem=k_ss.at[d], recv_sem=k_rs.at[d],
            device_id=(r, y * NK + 1 - k), device_id_type=MESH,
        )

    def y_copy(d):
        to = lax.rem(y + d, NY)
        return pltpu.make_async_remote_copy(
            src_ref=ysend.at[d], dst_ref=yrecv.at[d], send_sem=y_ss.at[d], recv_sem=y_rs.at[d],
            device_id=(r, to * NK + k), device_id_type=MESH,
        )

    def swap():
        for d in (2, 1, 3, 0):
            to = lax.rem(y + d, NY) * NK + 1 - k
            for i in range(RB):
                part[d, i] = run[last[i], to]
            part[d, 0, :, :128] = jnp.where(first, upart[to], part[d, 0, :, :128])
            k_copy(d).start()

    def share():
        for d in (2, 1, 3, 0):
            k_copy(d).wait_recv()
            to = lax.rem(y + d, NY) * NK + k
            for i in range(RB):
                total = run[last[i], to]
                if i == 0:
                    total = jnp.where(lane0, jnp.concatenate([upart[to]] * 2, axis=1), total)
                total = total + recvk[d, i]
                if d:
                    ysend[d, i] = total.astype(jnp.bfloat16)
                else:
                    image[i] = total
            if d:
                y_copy(d).start()

    lane0 = lax.broadcasted_iota(jnp.int32, (RHS, TILE), 1) == 0
    top()
    compute()
    swap()
    share()
    for d in (1, 3, 2):
        y_copy(d).wait_recv()
    for i in range(RB):
        total = image[i]
        for d in range(1, NY):
            total = total + yrecv[d, i].astype(jnp.float32)
        image[i] = total

    back = [image[i, :, :128] for i in range(RB)]
    stride = RB // 2
    while stride >= 1:
        for p in range(0, RB, 2 * stride):
            u, v = back[p], back[p + stride]
            back[p], back[p + stride] = (u + v) * ROOT_HALF, (u - v) * ROOT_HALF
        stride //= 2
    for i in range(RB):
        image[i, :, :128] = jnp.where(first, back[i], image[i, :, :128])
    coefs = jnp.concatenate([image[i] for i in range(RB)], axis=0)
    result = split_dot(coefs * fac_ref[...], s_ref[...])
    for b in range(RB):
        out_ref[:, b * TILE : (b + 1) * TILE] = result[b * RHS : (b + 1) * RHS]

    for level in range(LEVELS + 1):
        @pl.when(targets[level] != r)
        def _():
            f_copy(level, targets[level]).wait_send()
    for h in range(NPART):
        stage_a_done(h)
    for m, h in order:
        sends_done(m, h)
    for d in range(NY):
        k_copy(d).wait_send()
    for d in range(1, NY):
        y_copy(d).wait_send()
    owners(lambda copy: copy.wait_send())

    @pl.when(x == 0)
    def _():
        heirs(lambda copy: copy.wait_send())


def local(sources, tiles, tile_row, tile_col, tile_count):
    table, factor = sign_table(TILE)
    s_mat = jnp.asarray(table, jnp.bfloat16)
    st_mat = jnp.asarray(table.T.copy(), jnp.bfloat16)
    fac = jnp.asarray(factor[None, :], jnp.float32)
    vmem = pl.BlockSpec(memory_space=pltpu.VMEM)
    hbm = pl.BlockSpec(memory_space=pltpu.HBM)
    f32, b16 = jnp.float32, jnp.bfloat16
    dma = pltpu.SemaphoreType.DMA
    return pl.pallas_call(
        kernel,
        out_shape=jax.ShapeDtypeStruct((RHS, RB * TILE), f32),
        in_specs=[hbm] * 8,
        out_specs=vmem,
        scratch_shapes=[
            pltpu.SMEM((1, 1, SLOTS), jnp.int32),
            pltpu.SMEM((1, 1, SLOTS), jnp.int32),
            pltpu.SMEM((1, 1), jnp.int32),
            pltpu.VMEM((1, 1, SLOTS), jnp.int32),
            pltpu.VMEM((1, 1, SLOTS), jnp.int32),
            pltpu.VMEM((TILE, TILE), b16),
            pltpu.VMEM((TILE, TILE), b16),
            pltpu.VMEM((1, TILE), f32),
            pltpu.VMEM((RHS, RB * TILE), f32),
            pltpu.VMEM((SLOTS, TILE, TILE), b16),
            pltpu.VMEM((RB, RHS, TILE), b16),
            pltpu.VMEM((NCOL, NX * RB, RHS, TILE), b16),
            pltpu.VMEM((SLOTS + 1, NCOL, RHS, TILE), f32),
            pltpu.VMEM((NY, RB, RHS, TILE), f32),
            pltpu.VMEM((NY, RB, RHS, TILE), f32),
            pltpu.VMEM((NY, RB, RHS, TILE), b16),
            pltpu.VMEM((NY, RB, RHS, TILE), b16),
            pltpu.VMEM((RB, RHS, TILE), f32),
            pltpu.VMEM((RHS, 128), f32),
            pltpu.VMEM((NROW, RHS, 128), f32),
            pltpu.VMEM((RHS, 128), f32),
            pltpu.VMEM((NX * RB, TILE), f32),
            pltpu.VMEM((LEVELS + 2, NX * RB, TILE), f32),
            pltpu.VMEM((NX * RB, TILE), f32),
            pltpu.VMEM((NX * RB, TILE), f32),
            pltpu.VMEM((NCOL, RHS, 128), f32),
            pltpu.SMEM((SLOTS,), jnp.int32),
            pltpu.SMEM((RB,), jnp.int32),
            dma((10,)),
            dma((LEVELS + 1,)),
            dma((NROW,)),
            dma((NPART * NZ,)),
            dma((NPART * NCOL,)),
            dma((NPART,)),
            dma((NPART * 2 * NCOL,)),
            dma((NPART * 2 * NCOL,)),
            dma((NPART * NCOL,)),
            dma((NPART * NCOL,)),
            dma((NY,)),
            dma((NY,)),
            dma((NY,)),
            dma((NY,)),
            dma((NZ + NX,)),
            dma((LEVELS + 2,)),
        ],
        compiler_params=pltpu.CompilerParams(
            collective_id=0, has_side_effects=True, vmem_limit_bytes=64 * 2**20
        ),
    )(sources, tiles, tile_row, tile_col, tile_count, st_mat, s_mat, fac)


def solution(mesh):
    return jax.shard_map(
        local,
        mesh=mesh,
        in_specs=(
            P("col", "row"),
            P("row", "col", None, None, None),
            P("row", "col", None),
            P("row", "col", None),
            P("row", "col"),
        ),
        out_specs=P("col", "row"),
        check_vma=False,
    )
```

```python
import math

import jax
import jax.numpy as jnp
import numpy as np
from jax import lax
from jax.experimental import pallas as pl
from jax.experimental.pallas import tpu as pltpu
from jax.sharding import PartitionSpec as P

MESH = pl.DeviceIdType.MESH
ROOT_HALF = 1.0 / math.sqrt(2.0)
NX, NY, NZ, NK = 4, 4, 8, 2
NROW, NCOL = NX * NZ, NY * NK
TILE = 256
RHS = 16
RB = 8
SLOTS = 48
PARTS = ((4, 4), (0, 4))
NPART = len(PARTS)
LAG = 8
BEFORE = 2
CUTS = 4
MIDDLE = 6
LATER = 13


def direct(m, h):
    return h == NPART - 1 and m >= NCOL - 1


LEVELS = 5


def sign_table(extent):
    signs = np.zeros((extent, extent), np.float32)
    signs[0] = 1.0
    for n in range(1, extent):
        low = n & -n
        signs[n, n - low : n] = 1.0
        signs[n, n : n + low] = -1.0
    return signs


def split_dot(values, matrix):
    m = values.shape[0]
    hi = values.astype(jnp.bfloat16)
    rest = values - hi.astype(jnp.float32)
    mid = rest.astype(jnp.bfloat16)
    low = (rest - mid.astype(jnp.float32)).astype(jnp.bfloat16)
    stacked = jnp.concatenate([hi, mid, low], axis=0)
    out = jnp.dot(stacked, matrix, preferred_element_type=jnp.float32)
    return out[:m] + (out[m : 2 * m] + out[2 * m :])


def kernel(
    src_hbm, tiles_hbm, trow_hbm, tcol_hbm, tcnt_hbm, st_hbm, s_hbm,
    out_ref,
    trow, tcol, tcnt, trow_v, tcol_v, st_ref, s_ref,
    src, tiles, wav, xa, run, part, recvk, ysend, yrecv, image,
    fsend, frecv, facc, column, erecv, combo, full, picked, upart, prev, last,
    ld_sem, f_ss, f_rs, a_ss, a_rs, l_sem, b_ss, b_rs, r_ss, r_rs, k_ss, k_rs, y_ss, y_rs, e_ss, e_rs,
):
    r = lax.axis_index("row")
    c = lax.axis_index("col")
    x, z = lax.rem(r, NX), r // NX
    y, k = c // NK, lax.rem(c, NK)

    bar = pltpu.get_barrier_semaphore()

    def signal_row(j, carry):
        pl.semaphore_signal(bar, inc=1, device_id=(lax.rem(r + j, NROW), c), device_id_type=MESH)
        return carry

    lax.fori_loop(1, NROW, signal_row, 0)

    def signal_source(j, carry):
        @pl.when(jnp.logical_not(jnp.logical_and(z == c, j == c)))
        def _():
            pl.semaphore_signal(bar, inc=1, device_id=(c * NX + x, j), device_id_type=MESH)

        return carry

    lax.fori_loop(0, NCOL, signal_source, 0)
    pl.semaphore_signal(bar, inc=1, device_id=(r, y * NK + 1 - k), device_id_type=MESH)
    for d in range(1, NY):
        pl.semaphore_signal(bar, inc=1, device_id=(r, lax.rem(y + d, NY) * NK + k), device_id_type=MESH)

    pairs = (
        (trow_hbm, trow), (tcol_hbm, tcol), (tcnt_hbm, tcnt), (src_hbm, src), (st_hbm, st_ref),
        (s_hbm, s_ref), (tiles_hbm.at[0, 0], tiles), (trow_hbm, trow_v), (tcol_hbm, tcol_v),
    )
    loads = [pltpu.make_async_copy(a, b, ld_sem.at[i]) for i, (a, b) in enumerate(pairs)]
    for load in loads:
        load.start()
    for load in loads[:3]:
        load.wait()

    count = tcnt[0, 0]

    def chain(t, lasts):
        row = jnp.where(t < count, trow[0, 0, t], -1)
        before = jnp.int32(0)
        new = []
        for i in range(RB):
            hit = row == i
            before = jnp.where(hit, lasts[i], before)
            new.append(jnp.where(hit, t + 1, lasts[i]))
        prev[t] = before
        return tuple(new)

    lasts = lax.fori_loop(0, SLOTS, chain, tuple(jnp.int32(0) for _ in range(RB)))
    for i in range(RB):
        last[i] = lasts[i]
    run[0] = jnp.zeros((NCOL, RHS, TILE), jnp.float32)

    place = lax.broadcasted_iota(jnp.int32, (1, TILE), 1)
    factor = jnp.full((1, TILE), TILE**-0.5, jnp.float32)
    low = 1
    while low < TILE:
        factor = jnp.where(lax.rem(place, 2 * low) == low, (2.0 * low) ** -0.5, factor)
        low *= 2
    for load in loads[3:5]:
        load.wait()
    stacked = jnp.concatenate([src[:, b * TILE : (b + 1) * TILE] for b in range(RB)], axis=0)
    coef = split_dot(stacked, st_ref[...]) * factor
    blocks = [coef[b * RHS : (b + 1) * RHS] for b in range(RB)]
    coarse = [blocks[b][:, :128] for b in range(RB)]
    stride = 1
    while stride < RB:
        for p in range(0, RB, 2 * stride):
            u, v = coarse[p], coarse[p + stride]
            coarse[p], coarse[p + stride] = (u + v) * ROOT_HALF, (u - v) * ROOT_HALF
        stride *= 2
    first = lax.broadcasted_iota(jnp.int32, (RHS, 128), 1) == 0
    for b in range(RB):
        low = jnp.where(first, coarse[b], blocks[b][:, :128])
        wav[b, :, :128] = low.astype(jnp.bfloat16)
        wav[b, :, 128:] = blocks[b][:, 128:].astype(jnp.bfloat16)
    fsend[...] = coarse[0]

    pl.semaphore_wait(bar, NROW - 1 + NY + NCOL - jnp.where(z == c, 1, 0))

    def f_copy(level, target):
        return pltpu.make_async_remote_copy(
            src_ref=fsend, dst_ref=frecv.at[r], send_sem=f_ss.at[level], recv_sem=f_rs.at[r],
            device_id=(target, c), device_id_type=MESH,
        )

    targets = [(r // 2 ** (lv + 1)) * 2 ** (lv + 1) + 2**lv for lv in range(LEVELS)] + [r * 0]
    for level in reversed(range(LEVELS + 1)):
        @pl.when(targets[level] != r)
        def _():
            f_copy(level, targets[level]).start()

    def half(ref, h):
        return ref.at[pl.ds(PARTS[h][0], PARTS[h][1])]

    def piece(cs, xi, h):
        return xa.at[cs, pl.ds(xi * RB + PARTS[h][0], PARTS[h][1])]

    def wait_for(ref, sem):
        pltpu.make_async_copy(ref, ref, sem).wait()

    def stage_a(h):
        def send(j, carry):
            dz = lax.rem(c + j, NZ)
            to = lax.rem(z + dz, NZ)
            mine = jnp.logical_and(dz == 0, z == c)

            @pl.when(jnp.logical_not(mine))
            def _():
                pltpu.make_async_remote_copy(
                    src_ref=half(wav, h), dst_ref=piece(c, x, h),
                    send_sem=a_ss.at[h * NZ + j], recv_sem=a_rs.at[h * NCOL + c],
                    device_id=(to * NX + x, z), device_id_type=MESH,
                ).start()

            @pl.when(mine)
            def _():
                pltpu.make_async_copy(half(wav, h), piece(c, x, h), l_sem.at[h]).start()

            return carry

        lax.fori_loop(0, NZ, send, 0)

    def stage_a_done(h):
        for j in range(NZ):
            @pl.when(jnp.logical_not(jnp.logical_and(lax.rem(c + j, NZ) == 0, z == c)))
            def _():
                wait_for(half(wav, h), a_ss.at[h * NZ + j])

    def source(m):
        return lax.rem(z - c - m + 3 * NZ, NCOL)

    def b_copy(m, h, d):
        cs = source(m)
        i = (h * NCOL + cs) * 2 + d
        to = lax.rem(x + 1 + 2 * d, NX)
        return pltpu.make_async_remote_copy(
            src_ref=piece(cs, x, h), dst_ref=piece(cs, x, h), send_sem=b_ss.at[i], recv_sem=b_rs.at[i],
            device_id=(z * NX + to, c), device_id_type=MESH,
        )

    def r_copy(m, h):
        cs = source(m)
        i = h * NCOL + cs
        d = (m + h) % 2
        if direct(m, h):
            origin, to = x, lax.rem(x + 2, NX)
        else:
            origin, to = lax.rem(x + 3 - 2 * d, NX), lax.rem(x + 1 + 2 * d, NX)
        return pltpu.make_async_remote_copy(
            src_ref=piece(cs, origin, h), dst_ref=piece(cs, origin, h), send_sem=r_ss.at[i], recv_sem=r_rs.at[i],
            device_id=(z * NX + to, c), device_id_type=MESH,
        )

    def b_arrived(m, h, d):
        cs = source(m)
        wait_for(piece(cs, lax.rem(x + 3 - 2 * d, NX), h), b_rs.at[(h * NCOL + cs) * 2 + d])

    def serve(m, h):
        cs = source(m)
        local = jnp.logical_and(z == c, c == cs)

        @pl.when(local)
        def _():
            wait_for(piece(cs, x, h), l_sem.at[h])

        @pl.when(jnp.logical_not(local))
        def _():
            wait_for(piece(cs, x, h), a_rs.at[h * NCOL + cs])

        b_copy(m, h, 0).start()
        b_copy(m, h, 1).start()
        if direct(m, h):
            r_copy(m, h).start()

    def relay(m, h):
        if not direct(m, h):
            b_arrived(m, h, (m + h) % 2)
            r_copy(m, h).start()

    def finish(m, h):
        cs = source(m)
        if direct(m, h):
            b_arrived(m, h, (m + h) % 2)
        b_arrived(m, h, 1 - (m + h) % 2)
        wait_for(piece(cs, lax.rem(x + 2, NX), h), r_rs.at[h * NCOL + cs])

    def sends_done(m, h):
        b_copy(m, h, 0).wait_send()
        b_copy(m, h, 1).wait_send()
        r_copy(m, h).wait_send()

    order = [(m, h) for h in range(NPART) for m in range(NCOL)]

    def serve_range(lo, hi):
        for n in range(lo, hi):
            if n < len(order):
                serve(*order[n])
            if 0 <= n - LAG:
                relay(*order[n - LAG])

    for h in range(NPART - 1):
        stage_a(h)
    serve_range(0, BEFORE)

    for level in range(LEVELS + 1):
        size = 2 ** (level + 1) if level < LEVELS else NROW
        mine = (lax.rem(r, size) == 2**level) if level < LEVELS else (r == 0)

        @pl.when(mine)
        def _():
            base = (r // size) * size

            def arrive(j, carry):
                sender = base + j

                @pl.when(sender != r)
                def _():
                    pltpu.make_async_copy(fsend, frecv.at[sender], f_rs.at[sender]).wait()

                @pl.when(sender == r)
                def _():
                    frecv[r] = fsend[...]

                return carry

            lax.fori_loop(0, size, arrive, 0)
            total = jnp.zeros((RHS, 128), jnp.float32)
            for j in range(size):
                value = frecv[base + j]
                total = total - value if level < LEVELS and j >= size // 2 else total + value
            facc[...] = total * (size**-0.5)

    wav[0, :, :128] = jnp.where(first, facc[...], wav[0, :, :128].astype(jnp.float32)).astype(jnp.bfloat16)
    stage_a(NPART - 1)
    serve_range(BEFORE, MIDDLE - CUTS + 1)

    for load in loads[5:]:
        load.wait()
    slot_lane = lax.broadcasted_iota(jnp.int32, (TILE, 128), 1)

    def pick(t, found):
        value = tiles[t, :, :128].astype(jnp.float32)
        return jnp.where(slot_lane == t, jnp.broadcast_to(value[:, :1], (TILE, 128)), found)

    found = jnp.zeros((TILE, 128), jnp.float32)
    for cut in range(CUTS):
        found = lax.fori_loop(cut * SLOTS // CUTS, (cut + 1) * SLOTS // CUTS, pick, found)
        picked[...] = found
        if cut < CUTS - 1:
            serve_range(MIDDLE - CUTS + 1 + cut, MIDDLE - CUTS + 2 + cut)
        found = picked[...]
    slot = lax.broadcasted_iota(jnp.int32, (NX * RB, SLOTS), 1)
    block = lax.broadcasted_iota(jnp.int32, (NX * RB, SLOTS), 0)
    hit = (tcol_v[0] == block) & (trow_v[0] == 0) & (slot < count)
    column[...] = lax.dot_general(
        hit.astype(jnp.bfloat16), found[:, :SLOTS].astype(jnp.bfloat16), (((1,), (1,)), ((), ())),
        preferred_element_type=jnp.float32,
    )

    def e_copy(ref, slot, j, target):
        return pltpu.make_async_remote_copy(
            src_ref=ref, dst_ref=erecv.at[slot], send_sem=e_ss.at[j], recv_sem=e_rs.at[slot],
            device_id=(target, c), device_id_type=MESH,
        )

    def owners(act):
        for level in range(LEVELS + 1):
            size = 2 ** (level + 1) if level < LEVELS else NROW
            jump = 1 if level < 2 else NX
            mine = (lax.rem(r, size) == 2**level) if level < LEVELS else (r == 0)

            @pl.when(mine)
            def _():
                def each(j, carry):
                    base = (r // size) * size
                    act(e_copy(column, level, j, base + lax.rem(r - base + j * jump, size)))
                    return carry

                lax.fori_loop(1, size // jump, each, 0)

    def heirs(act):
        for j in range(1, NX):
            act(e_copy(combo, LEVELS + 1, NZ + j, r + j))

    def arrive(levels):
        for level in levels:
            @pl.when(targets[level] != r)
            def _():
                wait_for(erecv.at[level], e_rs.at[level])

            @pl.when(targets[level] == r)
            def _():
                erecv[level] = column[...]

    def weighted(levels):
        total = jnp.zeros((NX * RB, TILE), jnp.float32)
        for level in levels:
            size = 2 ** (level + 1) if level < LEVELS else NROW
            weight = size**-0.5
            if level < LEVELS:
                weight = jnp.where(lax.rem(r, size) < size // 2, weight, -weight)
            total = total + erecv[level] * weight
        return total

    owners(lambda copy: copy.start())
    serve_range(MIDDLE, LATER)

    @pl.when(x == 0)
    def _():
        arrive(range(2, LEVELS + 1))
        combo[...] = weighted(range(2, LEVELS + 1))
        heirs(lambda copy: copy.start())

    serve_range(LATER, len(order) + LAG)

    @pl.when(x != 0)
    def _():
        wait_for(erecv.at[LEVELS + 1], e_rs.at[LEVELS + 1])
        full[...] = erecv[LEVELS + 1]

    @pl.when(x == 0)
    def _():
        full[...] = combo[...]

    arrive(range(2))
    full[...] = full[...] + weighted(range(2))

    for m, h in order:
        finish(m, h)

    def top():
        def add(b, total):
            side = xa[:, pl.ds(b, 1)].reshape(NCOL * RHS, TILE).astype(jnp.float32)
            return total + side * full[pl.ds(b, 1), :]

        total = lax.fori_loop(0, NX * RB, add, jnp.zeros((NCOL * RHS, TILE), jnp.float32), unroll=4)
        value = jnp.sum(total, axis=1, keepdims=True)
        upart[...] = jnp.broadcast_to(value, (NCOL * RHS, 128)).reshape(NCOL, RHS, 128)

    def compute():
        def step(t, carry):
            side = xa[:, pl.ds(tcol[0, 0, t], 1)].reshape(NCOL * RHS, TILE)
            product = jnp.dot(side, tiles[t], preferred_element_type=jnp.float32)
            run[t + 1] = run[prev[t]] + product.reshape(NCOL, RHS, TILE)
            return carry

        lax.fori_loop(0, SLOTS, step, 0, unroll=16)

    def k_copy(d):
        return pltpu.make_async_remote_copy(
            src_ref=part.at[d], dst_ref=recvk.at[d], send_sem=k_ss.at[d], recv_sem=k_rs.at[d],
            device_id=(r, y * NK + 1 - k), device_id_type=MESH,
        )

    def y_copy(d):
        to = lax.rem(y + d, NY)
        return pltpu.make_async_remote_copy(
            src_ref=ysend.at[d], dst_ref=yrecv.at[d], send_sem=y_ss.at[d], recv_sem=y_rs.at[d],
            device_id=(r, to * NK + k), device_id_type=MESH,
        )

    def swap():
        for d in (2, 1, 3, 0):
            to = lax.rem(y + d, NY) * NK + 1 - k
            for i in range(RB):
                part[d, i] = run[last[i], to]
            part[d, 0, :, :128] = jnp.where(first, upart[to], part[d, 0, :, :128])
            k_copy(d).start()

    def share():
        for d in (2, 1, 3, 0):
            k_copy(d).wait_recv()
            to = lax.rem(y + d, NY) * NK + k
            for i in range(RB):
                total = run[last[i], to]
                if i == 0:
                    total = jnp.where(lane0, jnp.concatenate([upart[to]] * 2, axis=1), total)
                total = total + recvk[d, i]
                if d:
                    ysend[d, i] = total.astype(jnp.bfloat16)
                else:
                    image[i] = total
            if d:
                y_copy(d).start()

    lane0 = lax.broadcasted_iota(jnp.int32, (RHS, TILE), 1) == 0
    top()
    compute()
    swap()
    share()
    for d in (1, 3, 2):
        y_copy(d).wait_recv()
    for i in range(RB):
        total = image[i]
        for d in range(1, NY):
            total = total + yrecv[d, i].astype(jnp.float32)
        image[i] = total

    back = [image[i, :, :128] for i in range(RB)]
    stride = RB // 2
    while stride >= 1:
        for p in range(0, RB, 2 * stride):
            u, v = back[p], back[p + stride]
            back[p], back[p + stride] = (u + v) * ROOT_HALF, (u - v) * ROOT_HALF
        stride //= 2
    for i in range(RB):
        image[i, :, :128] = jnp.where(first, back[i], image[i, :, :128])
    coefs = jnp.concatenate([image[i] for i in range(RB)], axis=0)
    result = split_dot(coefs * factor, s_ref[...])
    for b in range(RB):
        out_ref[:, b * TILE : (b + 1) * TILE] = result[b * RHS : (b + 1) * RHS]

    for level in range(LEVELS + 1):
        @pl.when(targets[level] != r)
        def _():
            f_copy(level, targets[level]).wait_send()
    for h in range(NPART):
        stage_a_done(h)
    for m, h in order:
        sends_done(m, h)
    for d in range(NY):
        k_copy(d).wait_send()
    for d in range(1, NY):
        y_copy(d).wait_send()
    owners(lambda copy: copy.wait_send())

    @pl.when(x == 0)
    def _():
        heirs(lambda copy: copy.wait_send())


def local(sources, tiles, tile_row, tile_col, tile_count):
    table = sign_table(TILE)
    s_mat = jnp.asarray(table, jnp.bfloat16)
    st_mat = jnp.asarray(table.T.copy(), jnp.bfloat16)
    vmem = pl.BlockSpec(memory_space=pltpu.VMEM)
    hbm = pl.BlockSpec(memory_space=pltpu.HBM)
    f32, b16 = jnp.float32, jnp.bfloat16
    dma = pltpu.SemaphoreType.DMA
    return pl.pallas_call(
        kernel,
        out_shape=jax.ShapeDtypeStruct((RHS, RB * TILE), f32),
        in_specs=[hbm] * 7,
        out_specs=vmem,
        scratch_shapes=[
            pltpu.SMEM((1, 1, SLOTS), jnp.int32),
            pltpu.SMEM((1, 1, SLOTS), jnp.int32),
            pltpu.SMEM((1, 1), jnp.int32),
            pltpu.VMEM((1, 1, SLOTS), jnp.int32),
            pltpu.VMEM((1, 1, SLOTS), jnp.int32),
            pltpu.VMEM((TILE, TILE), b16),
            pltpu.VMEM((TILE, TILE), b16),
            pltpu.VMEM((RHS, RB * TILE), f32),
            pltpu.VMEM((SLOTS, TILE, TILE), b16),
            pltpu.VMEM((RB, RHS, TILE), b16),
            pltpu.VMEM((NCOL, NX * RB, RHS, TILE), b16),
            pltpu.VMEM((SLOTS + 1, NCOL, RHS, TILE), f32),
            pltpu.VMEM((NY, RB, RHS, TILE), f32),
            pltpu.VMEM((NY, RB, RHS, TILE), f32),
            pltpu.VMEM((NY, RB, RHS, TILE), b16),
            pltpu.VMEM((NY, RB, RHS, TILE), b16),
            pltpu.VMEM((RB, RHS, TILE), f32),
            pltpu.VMEM((RHS, 128), f32),
            pltpu.VMEM((NROW, RHS, 128), f32),
            pltpu.VMEM((RHS, 128), f32),
            pltpu.VMEM((NX * RB, TILE), f32),
            pltpu.VMEM((LEVELS + 2, NX * RB, TILE), f32),
            pltpu.VMEM((NX * RB, TILE), f32),
            pltpu.VMEM((NX * RB, TILE), f32),
            pltpu.VMEM((TILE, 128), f32),
            pltpu.VMEM((NCOL, RHS, 128), f32),
            pltpu.SMEM((SLOTS,), jnp.int32),
            pltpu.SMEM((RB,), jnp.int32),
            dma((9,)),
            dma((LEVELS + 1,)),
            dma((NROW,)),
            dma((NPART * NZ,)),
            dma((NPART * NCOL,)),
            dma((NPART,)),
            dma((NPART * 2 * NCOL,)),
            dma((NPART * 2 * NCOL,)),
            dma((NPART * NCOL,)),
            dma((NPART * NCOL,)),
            dma((NY,)),
            dma((NY,)),
            dma((NY,)),
            dma((NY,)),
            dma((NZ + NX,)),
            dma((LEVELS + 2,)),
        ],
        compiler_params=pltpu.CompilerParams(
            collective_id=0, has_side_effects=True, vmem_limit_bytes=55000 * 2**10
        ),
    )(sources, tiles, tile_row, tile_col, tile_count, st_mat, s_mat)


def solution(mesh):
    return jax.shard_map(
        local,
        mesh=mesh,
        in_specs=(
            P("col", "row"),
            P("row", "col", None, None, None),
            P("row", "col", None),
            P("row", "col", None),
            P("row", "col"),
        ),
        out_specs=P("col", "row"),
        check_vma=False,
    )
```

```python
import math

import jax
import jax.numpy as jnp
import numpy as np
from jax import lax
from jax.experimental import pallas as pl
from jax.experimental.pallas import tpu as pltpu
from jax.sharding import PartitionSpec as P

MESH = pl.DeviceIdType.MESH
ROOT_HALF = 1.0 / math.sqrt(2.0)
NX, NY, NZ, NK = 4, 4, 8, 2
NROW, NCOL = NX * NZ, NY * NK
TILE = 256
RHS = 16
RB = 8
SLOTS = 48
PARTS = ((4, 4), (0, 4))
NPART = len(PARTS)
LAG = 8
BEFORE = 1
CUTS = 4
MIDDLE = 6
LATER = 13


def direct(m, h):
    return h == NPART - 1 and m >= NCOL - 1


LEVELS = 5


def sign_table(extent):
    signs = np.zeros((extent, extent), np.float32)
    signs[0] = 1.0
    for n in range(1, extent):
        low = n & -n
        signs[n, n - low : n] = 1.0
        signs[n, n : n + low] = -1.0
    return signs


def split_dot(values, matrix):
    m = values.shape[0]
    hi = values.astype(jnp.bfloat16)
    rest = values - hi.astype(jnp.float32)
    mid = rest.astype(jnp.bfloat16)
    low = (rest - mid.astype(jnp.float32)).astype(jnp.bfloat16)
    stacked = jnp.concatenate([hi, mid, low], axis=0)
    out = jnp.dot(stacked, matrix, preferred_element_type=jnp.float32)
    return out[:m] + (out[m : 2 * m] + out[2 * m :])


def kernel(
    src_hbm, tiles_hbm, trow_hbm, tcol_hbm, tcnt_hbm, st_hbm, s_hbm,
    out_ref,
    trow, tcol, tcnt, trow_v, tcol_v, st_ref, s_ref,
    src, tiles, wav, xa, run, part, recvk, ysend, yrecv, image,
    fsend, frecv, facc, column, erecv, combo, full, picked, upart, prev, last,
    ld_sem, f_ss, f_rs, a_ss, a_rs, l_sem, b_ss, b_rs, r_ss, r_rs, k_ss, k_rs, y_ss, y_rs, e_ss, e_rs,
):
    r = lax.axis_index("row")
    c = lax.axis_index("col")
    x, z = lax.rem(r, NX), r // NX
    y, k = c // NK, lax.rem(c, NK)

    bar = pltpu.get_barrier_semaphore()

    def signal_row(j, carry):
        pl.semaphore_signal(bar, inc=1, device_id=(lax.rem(r + j, NROW), c), device_id_type=MESH)
        return carry

    lax.fori_loop(1, NROW, signal_row, 0)

    def signal_source(j, carry):
        @pl.when(jnp.logical_not(jnp.logical_and(z == c, j == c)))
        def _():
            pl.semaphore_signal(bar, inc=1, device_id=(c * NX + x, j), device_id_type=MESH)

        return carry

    lax.fori_loop(0, NCOL, signal_source, 0)
    pl.semaphore_signal(bar, inc=1, device_id=(r, y * NK + 1 - k), device_id_type=MESH)
    for d in range(1, NY):
        pl.semaphore_signal(bar, inc=1, device_id=(r, lax.rem(y + d, NY) * NK + k), device_id_type=MESH)

    pairs = (
        (trow_hbm, trow), (tcol_hbm, tcol), (tcnt_hbm, tcnt), (src_hbm, src), (st_hbm, st_ref),
        (s_hbm, s_ref), (tiles_hbm.at[0, 0], tiles), (trow_hbm, trow_v), (tcol_hbm, tcol_v),
    )
    loads = [pltpu.make_async_copy(a, b, ld_sem.at[i]) for i, (a, b) in enumerate(pairs)]
    for load in loads:
        load.start()
    for load in loads[:3]:
        load.wait()

    count = tcnt[0, 0]

    def chain(t, lasts):
        row = jnp.where(t < count, trow[0, 0, t], -1)
        before = jnp.int32(0)
        new = []
        for i in range(RB):
            hit = row == i
            before = jnp.where(hit, lasts[i], before)
            new.append(jnp.where(hit, t + 1, lasts[i]))
        prev[t] = before
        return tuple(new)

    lasts = lax.fori_loop(0, SLOTS, chain, tuple(jnp.int32(0) for _ in range(RB)))
    for i in range(RB):
        last[i] = lasts[i]
    run[0] = jnp.zeros((NCOL, RHS, TILE), jnp.float32)

    place = lax.broadcasted_iota(jnp.int32, (1, TILE), 1)
    factor = jnp.full((1, TILE), TILE**-0.5, jnp.float32)
    low = 1
    while low < TILE:
        factor = jnp.where(lax.rem(place, 2 * low) == low, (2.0 * low) ** -0.5, factor)
        low *= 2
    for load in loads[3:5]:
        load.wait()
    stacked = jnp.concatenate([src[:, b * TILE : (b + 1) * TILE] for b in range(RB)], axis=0)
    coef = split_dot(stacked, st_ref[...]) * factor
    blocks = [coef[b * RHS : (b + 1) * RHS] for b in range(RB)]
    coarse = [blocks[b][:, :128] for b in range(RB)]
    stride = 1
    while stride < RB:
        for p in range(0, RB, 2 * stride):
            u, v = coarse[p], coarse[p + stride]
            coarse[p], coarse[p + stride] = (u + v) * ROOT_HALF, (u - v) * ROOT_HALF
        stride *= 2
    first = lax.broadcasted_iota(jnp.int32, (RHS, 128), 1) == 0
    for b in range(RB):
        low = jnp.where(first, coarse[b], blocks[b][:, :128])
        wav[b, :, :128] = low.astype(jnp.bfloat16)
        wav[b, :, 128:] = blocks[b][:, 128:].astype(jnp.bfloat16)
    fsend[...] = coarse[0]

    pl.semaphore_wait(bar, NROW - 1 + NY + NCOL - jnp.where(z == c, 1, 0))

    def f_copy(level, target):
        return pltpu.make_async_remote_copy(
            src_ref=fsend, dst_ref=frecv.at[r], send_sem=f_ss.at[level], recv_sem=f_rs.at[r],
            device_id=(target, c), device_id_type=MESH,
        )

    targets = [(r // 2 ** (lv + 1)) * 2 ** (lv + 1) + 2**lv for lv in range(LEVELS)] + [r * 0]
    for level in reversed(range(LEVELS + 1)):
        @pl.when(targets[level] != r)
        def _():
            f_copy(level, targets[level]).start()

    def half(ref, h):
        return ref.at[pl.ds(PARTS[h][0], PARTS[h][1])]

    def piece(cs, xi, h):
        return xa.at[cs, pl.ds(xi * RB + PARTS[h][0], PARTS[h][1])]

    def wait_for(ref, sem):
        pltpu.make_async_copy(ref, ref, sem).wait()

    def stage_a(h):
        def send(j, carry):
            dz = lax.rem(c + j, NZ)
            to = lax.rem(z + dz, NZ)
            mine = jnp.logical_and(dz == 0, z == c)

            @pl.when(jnp.logical_not(mine))
            def _():
                pltpu.make_async_remote_copy(
                    src_ref=half(wav, h), dst_ref=piece(c, x, h),
                    send_sem=a_ss.at[h * NZ + j], recv_sem=a_rs.at[h * NCOL + c],
                    device_id=(to * NX + x, z), device_id_type=MESH,
                ).start()

            @pl.when(mine)
            def _():
                pltpu.make_async_copy(half(wav, h), piece(c, x, h), l_sem.at[h]).start()

            return carry

        lax.fori_loop(0, NZ, send, 0)

    def stage_a_done(h):
        for j in range(NZ):
            @pl.when(jnp.logical_not(jnp.logical_and(lax.rem(c + j, NZ) == 0, z == c)))
            def _():
                wait_for(half(wav, h), a_ss.at[h * NZ + j])

    def source(m):
        return lax.rem(z - c - m + 3 * NZ, NCOL)

    def b_copy(m, h, d):
        cs = source(m)
        i = (h * NCOL + cs) * 2 + d
        to = lax.rem(x + 1 + 2 * d, NX)
        return pltpu.make_async_remote_copy(
            src_ref=piece(cs, x, h), dst_ref=piece(cs, x, h), send_sem=b_ss.at[i], recv_sem=b_rs.at[i],
            device_id=(z * NX + to, c), device_id_type=MESH,
        )

    def r_copy(m, h):
        cs = source(m)
        i = h * NCOL + cs
        d = (m + h) % 2
        if direct(m, h):
            origin, to = x, lax.rem(x + 2, NX)
        else:
            origin, to = lax.rem(x + 3 - 2 * d, NX), lax.rem(x + 1 + 2 * d, NX)
        return pltpu.make_async_remote_copy(
            src_ref=piece(cs, origin, h), dst_ref=piece(cs, origin, h), send_sem=r_ss.at[i], recv_sem=r_rs.at[i],
            device_id=(z * NX + to, c), device_id_type=MESH,
        )

    def b_arrived(m, h, d):
        cs = source(m)
        wait_for(piece(cs, lax.rem(x + 3 - 2 * d, NX), h), b_rs.at[(h * NCOL + cs) * 2 + d])

    def serve(m, h):
        cs = source(m)
        local = jnp.logical_and(z == c, c == cs)

        @pl.when(local)
        def _():
            wait_for(piece(cs, x, h), l_sem.at[h])

        @pl.when(jnp.logical_not(local))
        def _():
            wait_for(piece(cs, x, h), a_rs.at[h * NCOL + cs])

        b_copy(m, h, 0).start()
        b_copy(m, h, 1).start()
        if direct(m, h):
            r_copy(m, h).start()

    def relay(m, h):
        if not direct(m, h):
            b_arrived(m, h, (m + h) % 2)
            r_copy(m, h).start()

    def finish(m, h):
        cs = source(m)
        if direct(m, h):
            b_arrived(m, h, (m + h) % 2)
        b_arrived(m, h, 1 - (m + h) % 2)
        wait_for(piece(cs, lax.rem(x + 2, NX), h), r_rs.at[h * NCOL + cs])

    def sends_done(m, h):
        b_copy(m, h, 0).wait_send()
        b_copy(m, h, 1).wait_send()
        r_copy(m, h).wait_send()

    order = [(m, h) for h in range(NPART) for m in range(NCOL)]

    def serve_range(lo, hi):
        for n in range(lo, hi):
            if n < len(order):
                serve(*order[n])
            if 0 <= n - LAG:
                relay(*order[n - LAG])

    for h in range(NPART - 1):
        stage_a(h)
    serve_range(0, BEFORE)

    for level in range(LEVELS + 1):
        size = 2 ** (level + 1) if level < LEVELS else NROW
        mine = (lax.rem(r, size) == 2**level) if level < LEVELS else (r == 0)

        @pl.when(mine)
        def _():
            base = (r // size) * size

            def arrive(j, carry):
                sender = base + j

                @pl.when(sender != r)
                def _():
                    pltpu.make_async_copy(fsend, frecv.at[sender], f_rs.at[sender]).wait()

                @pl.when(sender == r)
                def _():
                    frecv[r] = fsend[...]

                return carry

            lax.fori_loop(0, size, arrive, 0)
            total = jnp.zeros((RHS, 128), jnp.float32)
            for j in range(size):
                value = frecv[base + j]
                total = total - value if level < LEVELS and j >= size // 2 else total + value
            facc[...] = total * (size**-0.5)

    wav[0, :, :128] = jnp.where(first, facc[...], wav[0, :, :128].astype(jnp.float32)).astype(jnp.bfloat16)
    stage_a(NPART - 1)
    serve_range(BEFORE, MIDDLE - CUTS + 1)

    for load in loads[5:]:
        load.wait()
    slot_lane = lax.broadcasted_iota(jnp.int32, (TILE, 128), 1)

    def pick(t, found):
        value = tiles[t, :, :128].astype(jnp.float32)
        return jnp.where(slot_lane == t, jnp.broadcast_to(value[:, :1], (TILE, 128)), found)

    found = jnp.zeros((TILE, 128), jnp.float32)
    for cut in range(CUTS):
        found = lax.fori_loop(cut * SLOTS // CUTS, (cut + 1) * SLOTS // CUTS, pick, found)
        picked[...] = found
        if cut < CUTS - 1:
            serve_range(MIDDLE - CUTS + 1 + cut, MIDDLE - CUTS + 2 + cut)
        found = picked[...]
    slot = lax.broadcasted_iota(jnp.int32, (NX * RB, SLOTS), 1)
    block = lax.broadcasted_iota(jnp.int32, (NX * RB, SLOTS), 0)
    hit = (tcol_v[0] == block) & (trow_v[0] == 0) & (slot < count)
    column[...] = lax.dot_general(
        hit.astype(jnp.bfloat16), found[:, :SLOTS].astype(jnp.bfloat16), (((1,), (1,)), ((), ())),
        preferred_element_type=jnp.float32,
    )

    def e_copy(ref, slot, j, target):
        return pltpu.make_async_remote_copy(
            src_ref=ref, dst_ref=erecv.at[slot], send_sem=e_ss.at[j], recv_sem=e_rs.at[slot],
            device_id=(target, c), device_id_type=MESH,
        )

    def owners(act):
        for level in range(LEVELS + 1):
            size = 2 ** (level + 1) if level < LEVELS else NROW
            jump = 1 if level < 2 else NX
            mine = (lax.rem(r, size) == 2**level) if level < LEVELS else (r == 0)

            @pl.when(mine)
            def _():
                def each(j, carry):
                    base = (r // size) * size
                    act(e_copy(column, level, j, base + lax.rem(r - base + j * jump, size)))
                    return carry

                lax.fori_loop(1, size // jump, each, 0)

    def heirs(act):
        for j in range(1, NX):
            act(e_copy(combo, LEVELS + 1, NZ + j, r + j))

    def arrive(levels):
        for level in levels:
            @pl.when(targets[level] != r)
            def _():
                wait_for(erecv.at[level], e_rs.at[level])

            @pl.when(targets[level] == r)
            def _():
                erecv[level] = column[...]

    def weighted(levels):
        total = jnp.zeros((NX * RB, TILE), jnp.float32)
        for level in levels:
            size = 2 ** (level + 1) if level < LEVELS else NROW
            weight = size**-0.5
            if level < LEVELS:
                weight = jnp.where(lax.rem(r, size) < size // 2, weight, -weight)
            total = total + erecv[level] * weight
        return total

    owners(lambda copy: copy.start())
    serve_range(MIDDLE, LATER)

    @pl.when(x == 0)
    def _():
        arrive(range(2, LEVELS + 1))
        combo[...] = weighted(range(2, LEVELS + 1))
        heirs(lambda copy: copy.start())

    serve_range(LATER, len(order) + LAG)

    @pl.when(x != 0)
    def _():
        wait_for(erecv.at[LEVELS + 1], e_rs.at[LEVELS + 1])
        full[...] = erecv[LEVELS + 1]

    @pl.when(x == 0)
    def _():
        full[...] = combo[...]

    arrive(range(2))
    full[...] = full[...] + weighted(range(2))

    for m, h in order:
        finish(m, h)

    def top():
        def add(b, total):
            side = xa[:, pl.ds(b, 1)].reshape(NCOL * RHS, TILE).astype(jnp.float32)
            return total + side * full[pl.ds(b, 1), :]

        total = lax.fori_loop(0, NX * RB, add, jnp.zeros((NCOL * RHS, TILE), jnp.float32), unroll=4)
        value = jnp.sum(total, axis=1, keepdims=True)
        upart[...] = jnp.broadcast_to(value, (NCOL * RHS, 128)).reshape(NCOL, RHS, 128)

    def compute():
        def step(t, carry):
            side = xa[:, pl.ds(tcol[0, 0, t], 1)].reshape(NCOL * RHS, TILE)
            product = jnp.dot(side, tiles[t], preferred_element_type=jnp.float32)
            run[t + 1] = run[prev[t]] + product.reshape(NCOL, RHS, TILE)
            return carry

        lax.fori_loop(0, SLOTS, step, 0, unroll=16)

    def k_copy(d):
        return pltpu.make_async_remote_copy(
            src_ref=part.at[d], dst_ref=recvk.at[d], send_sem=k_ss.at[d], recv_sem=k_rs.at[d],
            device_id=(r, y * NK + 1 - k), device_id_type=MESH,
        )

    def y_copy(d):
        to = lax.rem(y + d, NY)
        return pltpu.make_async_remote_copy(
            src_ref=ysend.at[d], dst_ref=yrecv.at[d], send_sem=y_ss.at[d], recv_sem=y_rs.at[d],
            device_id=(r, to * NK + k), device_id_type=MESH,
        )

    def swap():
        for d in (2, 1, 3, 0):
            to = lax.rem(y + d, NY) * NK + 1 - k
            for i in range(RB):
                part[d, i] = run[last[i], to]
            part[d, 0, :, :128] = jnp.where(first, upart[to], part[d, 0, :, :128])
            k_copy(d).start()

    def share():
        for d in (2, 1, 3, 0):
            k_copy(d).wait_recv()
            to = lax.rem(y + d, NY) * NK + k
            for i in range(RB):
                total = run[last[i], to]
                if i == 0:
                    total = jnp.where(lane0, jnp.concatenate([upart[to]] * 2, axis=1), total)
                total = total + recvk[d, i]
                if d:
                    ysend[d, i] = total.astype(jnp.bfloat16)
                else:
                    image[i] = total
            if d:
                y_copy(d).start()

    lane0 = lax.broadcasted_iota(jnp.int32, (RHS, TILE), 1) == 0
    top()
    compute()
    swap()
    share()
    for d in (1, 3, 2):
        y_copy(d).wait_recv()
    for i in range(RB):
        total = image[i]
        for d in range(1, NY):
            total = total + yrecv[d, i].astype(jnp.float32)
        image[i] = total

    back = [image[i, :, :128] for i in range(RB)]
    stride = RB // 2
    while stride >= 1:
        for p in range(0, RB, 2 * stride):
            u, v = back[p], back[p + stride]
            back[p], back[p + stride] = (u + v) * ROOT_HALF, (u - v) * ROOT_HALF
        stride //= 2
    for i in range(RB):
        image[i, :, :128] = jnp.where(first, back[i], image[i, :, :128])
    coefs = jnp.concatenate([image[i] for i in range(RB)], axis=0)
    result = split_dot(coefs * factor, s_ref[...])
    for b in range(RB):
        out_ref[:, b * TILE : (b + 1) * TILE] = result[b * RHS : (b + 1) * RHS]

    for level in range(LEVELS + 1):
        @pl.when(targets[level] != r)
        def _():
            f_copy(level, targets[level]).wait_send()
    for h in range(NPART):
        stage_a_done(h)
    for m, h in order:
        sends_done(m, h)
    for d in range(NY):
        k_copy(d).wait_send()
    for d in range(1, NY):
        y_copy(d).wait_send()
    owners(lambda copy: copy.wait_send())

    @pl.when(x == 0)
    def _():
        heirs(lambda copy: copy.wait_send())


def local(sources, tiles, tile_row, tile_col, tile_count):
    table = sign_table(TILE)
    s_mat = jnp.asarray(table, jnp.bfloat16)
    st_mat = jnp.asarray(table.T.copy(), jnp.bfloat16)
    vmem = pl.BlockSpec(memory_space=pltpu.VMEM)
    hbm = pl.BlockSpec(memory_space=pltpu.HBM)
    f32, b16 = jnp.float32, jnp.bfloat16
    dma = pltpu.SemaphoreType.DMA
    return pl.pallas_call(
        kernel,
        out_shape=jax.ShapeDtypeStruct((RHS, RB * TILE), f32),
        in_specs=[hbm] * 7,
        out_specs=vmem,
        scratch_shapes=[
            pltpu.SMEM((1, 1, SLOTS), jnp.int32),
            pltpu.SMEM((1, 1, SLOTS), jnp.int32),
            pltpu.SMEM((1, 1), jnp.int32),
            pltpu.VMEM((1, 1, SLOTS), jnp.int32),
            pltpu.VMEM((1, 1, SLOTS), jnp.int32),
            pltpu.VMEM((TILE, TILE), b16),
            pltpu.VMEM((TILE, TILE), b16),
            pltpu.VMEM((RHS, RB * TILE), f32),
            pltpu.VMEM((SLOTS, TILE, TILE), b16),
            pltpu.VMEM((RB, RHS, TILE), b16),
            pltpu.VMEM((NCOL, NX * RB, RHS, TILE), b16),
            pltpu.VMEM((SLOTS + 1, NCOL, RHS, TILE), f32),
            pltpu.VMEM((NY, RB, RHS, TILE), f32),
            pltpu.VMEM((NY, RB, RHS, TILE), f32),
            pltpu.VMEM((NY, RB, RHS, TILE), b16),
            pltpu.VMEM((NY, RB, RHS, TILE), b16),
            pltpu.VMEM((RB, RHS, TILE), f32),
            pltpu.VMEM((RHS, 128), f32),
            pltpu.VMEM((NROW, RHS, 128), f32),
            pltpu.VMEM((RHS, 128), f32),
            pltpu.VMEM((NX * RB, TILE), f32),
            pltpu.VMEM((LEVELS + 2, NX * RB, TILE), f32),
            pltpu.VMEM((NX * RB, TILE), f32),
            pltpu.VMEM((NX * RB, TILE), f32),
            pltpu.VMEM((TILE, 128), f32),
            pltpu.VMEM((NCOL, RHS, 128), f32),
            pltpu.SMEM((SLOTS,), jnp.int32),
            pltpu.SMEM((RB,), jnp.int32),
            dma((9,)),
            dma((LEVELS + 1,)),
            dma((NROW,)),
            dma((NPART * NZ,)),
            dma((NPART * NCOL,)),
            dma((NPART,)),
            dma((NPART * 2 * NCOL,)),
            dma((NPART * 2 * NCOL,)),
            dma((NPART * NCOL,)),
            dma((NPART * NCOL,)),
            dma((NY,)),
            dma((NY,)),
            dma((NY,)),
            dma((NY,)),
            dma((NZ + NX,)),
            dma((LEVELS + 2,)),
        ],
        compiler_params=pltpu.CompilerParams(
            collective_id=0, has_side_effects=True, vmem_limit_bytes=55000 * 2**10
        ),
    )(sources, tiles, tile_row, tile_col, tile_count, st_mat, s_mat)


def solution(mesh):
    return jax.shard_map(
        local,
        mesh=mesh,
        in_specs=(
            P("col", "row"),
            P("row", "col", None, None, None),
            P("row", "col", None),
            P("row", "col", None),
            P("row", "col"),
        ),
        out_specs=P("col", "row"),
        check_vma=False,
    )
```
